128 devices in a mesh: group: 8 (over x_hi, z), blk: 16 (over y, x_lo, core).
Axes of the slice: x: 4 (x_hi: 2, x_lo: 2; x = x_hi * 2 + x_lo), y: 4, z: 4, core: 2. Of those that a mesh axis runs over, the one named last changes fastest.
Arguments:
- picture_embedding_unscaled: float32 [98304, 1024], P(('group', 'blk')), may hold values from -0.5 to 0.5
- caption_tower_outputs: bfloat16 [98304, 1280], P(('group', 'blk')), may hold values from -6 to 6
- caption_mapping_matrix: bfloat16 [1280, 1024], replicated, may hold values from -0.15625 to 0.15625
- matching_caption_index: int32 [98304], P(('group', 'blk')), may hold values from 0 to 98303, as said below
- similarity_scaling: float32 [1], replicated, may hold values from 48 to 80
- score_offset: float32 [1], replicated, may hold values from -9.5 to -7.5
Outputs:
- grad_image: float32 [98304, 1024], P(('group', 'blk'))
- grad_proj: float32 [1280, 1024], replicated
The draws below stay inside these ranges and needn't reach their ends.
Inputs may be any that keep to these rules, and one draw needn't show every extreme that they name: `matching_caption_index`: the positive of image row i of block (g, k) lies in one of the text blocks paired with that image block in the window: (g, k - s mod 16) for some s from 0 to 1, or (g - 1 mod 8, k - 1 mod 16).
All inputs are finite; a program needn't handle non-finite values.
Results may differ from the reference program's by a relative error of at most 0.0063.
Values may be sent and summed in bfloat16 or wider, within the bound.
A program may use at most 128 MiB of HBM per device.

```python
import jax
import jax.numpy as jnp
from jax import lax

E = 1024
FT = 1280
TOK_DEV = 768
STEPS = 1
GROUPS = 8
CYCLE = 16
TOKENS = 98304


def draw_matching_caption_index(key, part):
    key = jax.random.fold_in(key, 7)
    key_offset, key_inner = jax.random.split(key)
    blocks = GROUPS * CYCLE
    offsets = jax.random.randint(key_offset, (blocks, TOK_DEV), 0, STEPS + 2)
    inner = jax.random.randint(key_inner, (blocks, TOK_DEV), 0, TOK_DEV)
    block_ids = jnp.arange(blocks, dtype=jnp.int32)[:, None]
    group_ids = block_ids // CYCLE
    rotation_identifiers = block_ids % CYCLE
    shifted_texts = offsets == STEPS + 1
    source_group = jnp.where(shifted_texts, (group_ids - 1) % GROUPS, group_ids)
    source_cycle = jnp.where(shifted_texts, (rotation_identifiers - STEPS) % CYCLE, (rotation_identifiers - offsets) % CYCLE)
    chosen = (source_group * CYCLE + source_cycle) * TOK_DEV + inner
    return chosen.reshape(-1).astype(jnp.int32)


def level_of(rng, dims, cuts, low, largest):
    gain, own = 1.0, jax.random.fold_in(rng, 6)
    for dim, shards_of in cuts:
        steps = jnp.exp(jax.random.uniform(jax.random.fold_in(own, dim), (shards_of,), jnp.float32, low / len(cuts), largest / len(cuts)))
        gain = gain * jnp.repeat(steps, dims[dim] // shards_of).reshape([-1 if axis == dim else 1 for axis in range(len(dims))])
    return gain


def noise(own_key, shape, deviation, reach, cuts=(), held_as=jnp.bfloat16):
    result = jax.random.normal(own_key, shape, jnp.float32) * deviation
    if len(cuts) > 0:
        result = level_of(own_key, shape, cuts, -0.22, 0.18) * result
    return jnp.clip(result, min=-reach, max=reach).astype(held_as)


def setup_inputs(seed: int = 0) -> dict:
    keys = jax.random.split(jax.random.key(seed), 7)
    picture_embedding_unscaled = noise(keys[0], (TOKENS, E), 0.03125, 0.5, ((0, 128),), jnp.float32)
    caption_tower_outputs = noise(keys[1], (TOKENS, FT), 1.0, 6.0, ((0, 128),))
    caption_mapping_matrix = noise(keys[2], (FT, E), FT ** -0.5, 0.15625)
    matching_caption_index = draw_matching_caption_index(jax.random.fold_in(keys[6], 71), 0)
    similarity_scaling = jnp.clip(jax.random.uniform(keys[4], (1,), jnp.float32, 48.0, 80.0), 48.0, 80.0)
    score_offset = jnp.clip(jax.random.uniform(keys[5], (1,), jnp.float32, -9.5, -7.5), -9.5, -7.5)
    return {"picture_embedding_unscaled": picture_embedding_unscaled, "caption_tower_outputs": caption_tower_outputs, "caption_mapping_matrix": caption_mapping_matrix, "matching_caption_index": matching_caption_index, "similarity_scaling": similarity_scaling, "score_offset": score_offset}


epsilon = 1e-06

def unit_rows(values):
    scale = jnp.sqrt(lax.optimization_barrier(jnp.sum(values * values, axis=-1, keepdims=True)) + epsilon)
    return (values / scale, scale)

def pair_terms(image_unit, text_block, matching_caption_index, columns, similarity_factor, logit_shift):
    logits = similarity_factor * jnp.dot(image_unit, text_block.T, preferred_element_type=jnp.float32) + logit_shift
    labels = jnp.where(matching_caption_index[:, None] == columns[None, :], 1.0, -1.0).astype(jnp.float32)
    weight = (-labels * jax.nn.sigmoid(-labels * logits)).astype(jnp.bfloat16)
    image_grad = similarity_factor * jnp.dot(weight, text_block, preferred_element_type=jnp.float32)
    text_grad = similarity_factor * jnp.dot(weight.T, image_unit, preferred_element_type=jnp.float32)
    return (image_grad, text_grad)

def reference(picture_embedding_unscaled, caption_tower_outputs, caption_mapping_matrix, matching_caption_index, similarity_scaling, score_offset):
    similarity_factor = similarity_scaling[0]
    logit_shift = score_offset[0]
    image_unit32, image_scale = unit_rows(picture_embedding_unscaled)
    image_unit = image_unit32.astype(jnp.bfloat16)
    projected = jnp.dot(caption_tower_outputs, caption_mapping_matrix, preferred_element_type=jnp.float32)
    text_unit32, text_scale = unit_rows(projected)
    text_unit = text_unit32.astype(jnp.bfloat16)
    blocks = GROUPS * CYCLE
    image_blocks = image_unit.reshape(blocks, TOK_DEV, E)
    text_grid = text_unit.reshape(GROUPS, CYCLE, TOK_DEV, E)
    column_grid = jnp.arange(TOKENS, dtype=jnp.int32).reshape(GROUPS, CYCLE, TOK_DEV)
    positive_blocks = matching_caption_index.reshape(blocks, TOK_DEV)
    image_grad = jnp.zeros((blocks, TOK_DEV, E), jnp.float32)
    text_grad = jnp.zeros((GROUPS, CYCLE, TOK_DEV, E), jnp.float32)
    offsets = [(0, offset) for offset in range(STEPS + 1)] + [(1, STEPS)]

    def single_block_view(items):
        return pair_terms(items[0], items[1], items[2], items[3], similarity_factor, logit_shift)
    for group_move, cycle_move in offsets:
        seen_text = jnp.roll(text_grid, (group_move, cycle_move), axis=(0, 1)).reshape(blocks, TOK_DEV, E)
        seen_columns = jnp.roll(column_grid, (group_move, cycle_move), axis=(0, 1)).reshape(blocks, TOK_DEV)
        image_part, text_part = lax.map(single_block_view, (image_blocks, seen_text, positive_blocks, seen_columns))
        image_grad = image_grad + image_part
        text_part = text_part.reshape(GROUPS, CYCLE, TOK_DEV, E)
        text_grad = text_grad + jnp.roll(text_part, (-group_move, -cycle_move), axis=(0, 1))
    image_grad = image_grad.reshape(TOKENS, E)
    text_grad = text_grad.reshape(TOKENS, E)
    grad_image = (image_grad - image_unit32 * lax.optimization_barrier(jnp.sum(image_unit32 * image_grad, axis=-1, keepdims=True))) / image_scale
    grad_projected = ((text_grad - text_unit32 * lax.optimization_barrier(jnp.sum(text_unit32 * text_grad, axis=-1, keepdims=True))) / text_scale).astype(jnp.bfloat16)
    grad_proj = jnp.dot(caption_tower_outputs.T, grad_projected, preferred_element_type=jnp.float32)
    return (grad_image, grad_proj)
```

```python
import jax
import jax.numpy as jnp
from jax import lax
from jax.experimental import pallas as pl
from jax.experimental.pallas import tpu as pltpu
from jax.sharding import PartitionSpec as P

EPS = 1e-06
ROWS = 768
E = 1024
FT = 1280
SEND = 128
SENDS = ROWS // SEND
TILE = 256
TILES = ROWS // TILE
HALF = E // 2
MESH = pl.DeviceIdType.MESH
BF16 = jnp.bfloat16
F32 = jnp.float32

PARTS = ((0, 32, "yxz"), (512, 32, "zyx"), (1024, 16, "xzy"))


def start_copy(src, dst, send, recv, device):
    pltpu.make_async_remote_copy(
        src_ref=src, dst_ref=dst, send_sem=send, recv_sem=recv, device_id=device, device_id_type=MESH
    ).start()


def wait_sent(src, send):
    pltpu.make_async_copy(src, src, send).wait()


def wait_got(dst, recv):
    pltpu.make_async_copy(dst, dst, recv).wait()


def kernel(
    scale_ref, bias_ref, index_ref, pic_hbm, cap_hbm, head_hbm,
    gi_ref, out_ref,
    pic, cap, head, iu, tu, tu32, trs, cap_t, i2, i3, t2, t3, idx, idx2, idx3, idx_col,
    w, g_text, g_image, gp, hs, r0, d, r1a, r1b, r1c, e_a, e_b, e_c, r2a, r2b, r2c, f_a, f_b, f_c, r3a, r3b, r3c,
    load_sem, is2, ir2, is3, ir3, is3r, ts2, tr2, ts3, tr3, ts3r, xs2, xr2, xs3, xr3,
    s0s, s0r, rs_s, rs_r, ag_s, ag_r, a0s, a0r,
):
    g = lax.axis_index("group")
    k = lax.axis_index("blk")
    z = g % 4
    y = k // 4
    x = (g // 4) * 2 + (k // 2) % 2
    core = k % 2
    odd = core == 1
    even = core == 0
    place = {"x": x, "y": y, "z": z}

    def device(xx, yy, zz, cc):
        return ((xx // 2) * 4 + zz, yy * 4 + (xx % 2) * 2 + cc)

    def on_axis(axis, d):
        p = dict(place)
        p[axis] = (p[axis] + d) % 4
        return device(p["x"], p["y"], p["z"], core)

    def shift(dg, dk):
        return ((g + dg + 8) % 8, (k + dk + 16) % 16)

    other_core = device(x, y, z, 1 - core)

    loads = []
    for c in range(SENDS):
        loads.append(pltpu.make_async_copy(pic_hbm.at[pl.ds(c * SEND, SEND)], pic.at[pl.ds(c * SEND, SEND)], load_sem.at[c]))
    loads.append(pltpu.make_async_copy(cap_hbm, cap, load_sem.at[SENDS]))
    loads.append(pltpu.make_async_copy(head_hbm, head, load_sem.at[SENDS + 1]))
    for load in loads:
        load.start()

    barrier = pltpu.get_barrier_semaphore()
    partners = [shift(0, 1), shift(0, -1), shift(1, 0), shift(-1, 0), shift(1, 1), shift(-1, -1), other_core]
    for axis in "xyz":
        for step in (1, 2, 3):
            partners.append(on_axis(axis, step))
    for p in partners:
        pl.semaphore_signal(barrier, inc=1, device_id=p, device_id_type=MESH)

    scale = scale_ref[0]
    bias = bias_ref[0]

    idx[...] = jnp.broadcast_to(index_ref[...], (8, ROWS))

    def normalize_image(c, _):
        r = pl.ds(pl.multiple_of(c * SEND, SEND), SEND)
        pltpu.make_async_copy(pic.at[r], pic.at[r], load_sem.at[c]).wait()
        v = pic[r, :]
        inv = lax.rsqrt(jnp.sum(v * v, axis=1, keepdims=True) + EPS)
        iu[r, :] = (v * inv).astype(BF16)
        return 0

    lax.fori_loop(0, SENDS, normalize_image, 0)
    pl.semaphore_wait(barrier, len(partners))

    direct_image = jnp.logical_or(odd, z == 0)
    direct_text = jnp.logical_or(even, z == 3)
    down = shift(0, -1)
    cross_down = shift(-1, -1)
    start_copy(idx, idx2, xs2, xr2, down)
    start_copy(idx, idx3, xs3, xr3, cross_down)

    def send_images(c, _):
        r = pl.ds(pl.multiple_of(c * SEND, SEND), SEND)
        start_copy(iu.at[r], i2.at[r], is2.at[c], ir2.at[c], down)

        @pl.when(direct_image)
        def _():
            start_copy(iu.at[r], i3.at[r], is3.at[c], ir3.at[c], cross_down)

        return 0

    lax.fori_loop(0, SENDS, send_images, 0)

    loads[SENDS].wait()
    loads[SENDS + 1].wait()

    def project(n, _):
        cols = pl.ds(pl.multiple_of(n * TILE, TILE), TILE)
        tu32[:, cols] = jnp.dot(cap[...], head[:, cols], preferred_element_type=F32)
        return 0

    lax.fori_loop(0, E // TILE, project, 0)

    def normalize_text(c, _):
        r = pl.ds(pl.multiple_of(c * SEND, SEND), SEND)
        v = tu32[r, :]
        inv = lax.rsqrt(jnp.sum(v * v, axis=1, keepdims=True) + EPS)
        u = v * inv
        tu32[r, :] = u
        tu[r, :] = u.astype(BF16)
        trs[r, :] = jnp.broadcast_to(inv, (SEND, 128))
        return 0

    lax.fori_loop(0, SENDS, normalize_text, 0)
    up = shift(0, 1)
    cross_up = shift(1, 1)

    def send_texts(c, _):
        r = pl.ds(pl.multiple_of(c * SEND, SEND), SEND)
        start_copy(tu.at[r], t2.at[r], ts2.at[c], tr2.at[c], up)

        @pl.when(direct_text)
        def _():
            start_copy(tu.at[r], t3.at[r], ts3.at[c], tr3.at[c], cross_up)

        return 0

    lax.fori_loop(0, SENDS, send_texts, 0)

    for c in range(ROWS // 128):
        row = jnp.broadcast_to(index_ref[0:1, pl.ds(c * 128, 128)], (128, 128))
        idx_col[pl.ds(c * 128, 128), :] = row.T

    own_first = (g * 16 + k) * ROWS

    def weights(logits, match):
        v = logits * scale + bias
        v = jnp.where(match, -v, v)
        s = 1.0 / (1.0 + jnp.exp(-v))
        return jnp.where(match, -s, s).astype(BF16)

    def text_logits(c, images, index):
        r = pl.ds(pl.multiple_of(c * TILE, TILE), TILE)
        logits = lax.dot_general(tu[...], images[r, :], (((1,), (1,)), ((), ())), preferred_element_type=F32)
        match = (index[0:1, r] - own_first) == lax.broadcasted_iota(jnp.int32, (ROWS, TILE), 0)
        w[:, r] = weights(logits, match)

    def image_logits(c, texts, first):
        r = pl.ds(pl.multiple_of(c * TILE, TILE), TILE)
        logits = lax.dot_general(iu[...], texts[r, :], (((1,), (1,)), ((), ())), preferred_element_type=F32)
        column = idx_col[...] - (first + c * TILE)
        column = jnp.concatenate([column, column - 128], axis=1)
        match = column == (lax.broadcasted_iota(jnp.int32, (ROWS, TILE), 1) % 128)
        w[:, r] = weights(logits, match)

    def add_grad(total, block, first):
        def step(n, _):
            cols = pl.ds(pl.multiple_of(n * TILE, TILE), TILE)
            term = jnp.dot(w[...], block[:, cols], preferred_element_type=F32)
            total[:, cols] = term if first else total[:, cols] + term
            return 0

        lax.fori_loop(0, E // TILE, step, 0)

    def text_side(images, index, first, before):
        def step(c, _):
            before(c)
            text_logits(c, images, index)
            return 0

        lax.fori_loop(0, TILES, step, 0)
        add_grad(g_text, images, first)

    def image_side(texts, first_row, first, before):
        def step(c, _):
            before(c)
            image_logits(c, texts, first_row)
            return 0

        lax.fori_loop(0, TILES, step, 0)
        add_grad(g_image, texts, first)

    def nothing(c):
        pass

    per = TILE // SEND

    def got(buffer, sems, forward):
        def before(c):
            for i in range(per):
                m = c * per + i
                r = pl.ds(pl.multiple_of(m * SEND, SEND), SEND)
                wait_got(buffer.at[r], sems.at[m])
                forward(m, r)

        return before

    def no_forward(m, r):
        pass

    forward_image = jnp.logical_and(odd, z != 0)
    forward_text = jnp.logical_and(even, z != 3)

    def pass_image(m, r):
        @pl.when(forward_image)
        def _():
            start_copy(i2.at[r], i3.at[r], is3r.at[m], ir3.at[m], shift(-1, 0))

    def pass_text(m, r):
        @pl.when(forward_text)
        def _():
            start_copy(t2.at[r], t3.at[r], ts3r.at[m], tr3.at[m], shift(1, 0))

    text_side(iu, idx, True, nothing)
    image_side(tu, own_first, True, nothing)

    def turn(n, _):
        cols = pl.ds(pl.multiple_of(n * TILE, TILE), TILE)
        for m in range(TILES):
            cap_t[cols, pl.ds(m * TILE, TILE)] = cap[pl.ds(m * TILE, TILE), cols].T
        return 0

    lax.fori_loop(0, FT // TILE, turn, 0)

    wait_got(idx2, xr2)
    text_side(i2, idx2, False, got(i2, ir2, pass_image))
    before_t2 = got(t2, tr2, pass_text)

    def step_t2(c, _):
        before_t2(c)
        return 0

    lax.fori_loop(0, TILES, step_t2, 0)
    wait_got(idx3, xr3)
    text_side(i3, idx3, False, got(i3, ir3, no_forward))

    def finish_text(c, _):
        r = pl.ds(pl.multiple_of(c * SEND, SEND), SEND)
        u = tu32[r, :]
        v = g_text[r, :] * scale
        dot = jnp.sum(u * v, axis=1, keepdims=True)
        gp[r, :] = ((v - u * dot) * trs[r, 0:1]).astype(BF16)
        return 0

    lax.fori_loop(0, SENDS, finish_text, 0)

    r1 = (r1a, r1b, r1c)
    e_ = (e_a, e_b, e_c)
    r2 = (r2a, r2b, r2c)
    f_ = (f_a, f_b, f_c)
    r3 = (r3a, r3b, r3c)
    mine = pl.multiple_of(core * HALF, HALF)
    theirs = pl.multiple_of((1 - core) * HALF, HALF)

    def span(p):
        base, own, _ = PARTS[p]
        return pl.ds(base, 16 * own)

    for p in range(3):
        rows = span(p)
        for n in range(HALF // TILE):
            hs[rows, pl.ds(n * TILE, TILE)] = jnp.dot(
                cap_t[rows, :], gp[:, pl.ds(pl.multiple_of(theirs + n * TILE, TILE), TILE)], preferred_element_type=F32
            ).astype(BF16)
        start_copy(hs.at[rows], r0.at[rows], s0s.at[p], s0r.at[p], other_core)

    for p in range(3):
        base, own, order = PARTS[p]
        rows = span(p)
        for n in range(HALF // TILE):
            term = jnp.dot(
                cap_t[rows, :], gp[:, pl.ds(pl.multiple_of(mine + n * TILE, TILE), TILE)], preferred_element_type=F32
            )
            if n == 0:
                wait_got(r0.at[rows], s0r.at[p])
            cols = pl.ds(n * TILE, TILE)
            d[rows, cols] = (term + r0[rows, cols].astype(F32)).astype(BF16)
        i = place[order[0]]
        for s in (1, 2, 3):
            j = (i + s) % 4
            start_copy(
                d.at[pl.ds(pl.multiple_of(base + j * 4 * own, 16), 4 * own)],
                r1[p].at[s - 1], rs_s.at[p, 0, s - 1], rs_r.at[p, 0, s - 1], on_axis(order[0], s),
            )

    def total(own, parts):
        v = own.astype(F32)
        for s in range(3):
            v = v + parts[s].astype(F32)
        return v.astype(BF16)

    image_side(t2, (g * 16 + (k + 15) % 16) * ROWS, False, nothing)

    for p in range(3):
        base, own, order = PARTS[p]
        for s in range(3):
            wait_got(r1[p].at[s], rs_r.at[p, 0, s])
        i = place[order[0]]
        e_[p][...] = total(d[pl.ds(pl.multiple_of(base + i * 4 * own, 16), 4 * own), :], [r1[p][s] for s in range(3)])
        i = place[order[1]]
        for s in (1, 2, 3):
            j = (i + s) % 4
            start_copy(
                e_[p].at[pl.ds(pl.multiple_of(j * own, 16), own)],
                r2[p].at[s - 1], rs_s.at[p, 1, s - 1], rs_r.at[p, 1, s - 1], on_axis(order[1], s),
            )
    for p in range(3):
        base, own, order = PARTS[p]
        for s in range(3):
            wait_got(r2[p].at[s], rs_r.at[p, 1, s])
        i = place[order[1]]
        f_[p][...] = total(e_[p][pl.ds(pl.multiple_of(i * own, 16), own), :], [r2[p][s] for s in range(3)])
        i = place[order[2]]
        for s in (1, 2, 3):
            j = (i + s) % 4
            start_copy(
                f_[p].at[:, pl.ds(pl.multiple_of(j * 128, 128), 128)],
                r3[p].at[s - 1], rs_s.at[p, 2, s - 1], rs_r.at[p, 2, s - 1], on_axis(order[2], s),
            )

    def block(p, a, b, c):
        base, own, _ = PARTS[p]
        if a is None:
            rows = pl.ds(base, 16 * own)
        elif b is None:
            rows = pl.ds(pl.multiple_of(base + a * 4 * own, 16), 4 * own)
        else:
            rows = pl.ds(pl.multiple_of(base + (a * 4 + b) * own, 16), own)
        if c is None:
            cols = pl.ds(mine, HALF)
        else:
            cols = pl.ds(pl.multiple_of(mine + c * 128, 128), 128)
        return rows, cols

    def gather(p, stage, rows, cols):
        axis = PARTS[p][2][stage]
        for s in (1, 2, 3):
            ref = out_ref.at[rows, cols]
            start_copy(ref, ref, ag_s.at[p, stage, s - 1], ag_r.at[p, stage, s - 1], on_axis(axis, s))

    def seat(p):
        order = PARTS[p][2]
        return [place[a] for a in order]

    for p in range(3):
        a, b, c = seat(p)
        for s in range(3):
            wait_got(r3[p].at[s], rs_r.at[p, 2, s])
        rows, cols = block(p, a, b, c)
        out_ref[rows, cols] = total(f_[p][:, pl.ds(pl.multiple_of(c * 128, 128), 128)], [r3[p][s] for s in range(3)])
        gather(p, 2, rows, cols)
    for p in range(3):
        a, b, c = seat(p)
        for s in (1, 2, 3):
            wait_got(out_ref.at[block(p, a, b, (c - s + 4) % 4)], ag_r.at[p, 2, s - 1])
        gather(p, 1, *block(p, a, b, None))
    for p in range(3):
        a, b, c = seat(p)
        for s in (1, 2, 3):
            wait_got(out_ref.at[block(p, a, (b - s + 4) % 4, None)], ag_r.at[p, 1, s - 1])
        gather(p, 0, *block(p, a, None, None))
        ref = out_ref.at[block(p, a, None, None)]
        start_copy(ref, ref, a0s.at[p, 0], a0r.at[p, 0], other_core)

    image_side(t3, (((g + 7) % 8) * 16 + (k + 15) % 16) * ROWS, False, got(t3, tr3, no_forward))

    def finish_image(c, _):
        r = pl.ds(pl.multiple_of(c * SEND, SEND), SEND)
        u = pic[r, :]
        inv = lax.rsqrt(jnp.sum(u * u, axis=1, keepdims=True) + EPS)
        u = u * inv
        v = g_image[r, :] * scale
        dot = jnp.sum(u * v, axis=1, keepdims=True)
        gi_ref[r, :] = ((v - u * dot) * inv).astype(BF16)
        return 0

    lax.fori_loop(0, SENDS, finish_image, 0)

    for p in range(3):
        a, b, c = seat(p)
        for s in (1, 2, 3):
            ref = out_ref.at[block(p, (a - s + 4) % 4, None, None)]
            wait_got(ref, ag_r.at[p, 0, s - 1])
            start_copy(ref, ref, a0s.at[p, s], a0r.at[p, s], other_core)
    for p in range(3):
        base, own, _ = PARTS[p]
        a, b, c = seat(p)
        for s in range(4):
            rows = pl.ds(pl.multiple_of(base + ((a - s + 4) % 4) * 4 * own, 16), 4 * own)
            wait_got(out_ref.at[rows, pl.ds(theirs, HALF)], a0r.at[p, s])

    wait_sent(idx, xs2)
    wait_sent(idx, xs3)

    def drain(c, _):
        r = pl.ds(pl.multiple_of(c * SEND, SEND), SEND)
        wait_sent(iu.at[r], is2.at[c])
        wait_sent(tu.at[r], ts2.at[c])

        @pl.when(direct_image)
        def _():
            wait_sent(iu.at[r], is3.at[c])

        @pl.when(direct_text)
        def _():
            wait_sent(tu.at[r], ts3.at[c])

        @pl.when(forward_image)
        def _():
            wait_sent(i2.at[r], is3r.at[c])

        @pl.when(forward_text)
        def _():
            wait_sent(t2.at[r], ts3r.at[c])

        return 0

    lax.fori_loop(0, SENDS, drain, 0)
    for p in range(3):
        base, own, _ = PARTS[p]
        a, b, c = seat(p)
        wait_sent(hs.at[span(p)], s0s.at[p])
        for s in range(3):
            wait_sent(r1[p].at[s], rs_s.at[p, 0, s])
            wait_sent(r2[p].at[s], rs_s.at[p, 1, s])
            wait_sent(r3[p].at[s], rs_s.at[p, 2, s])
            wait_sent(out_ref.at[block(p, a, b, c)], ag_s.at[p, 2, s])
            wait_sent(out_ref.at[block(p, a, b, None)], ag_s.at[p, 1, s])
            wait_sent(out_ref.at[block(p, a, None, None)], ag_s.at[p, 0, s])
        for s in range(4):
            wait_sent(out_ref.at[block(p, (a - s + 4) % 4, None, None)], a0s.at[p, s])


def scratch():
    vmem = pltpu.VMEM
    dma = pltpu.SemaphoreType.DMA
    block = vmem((ROWS, E), BF16)
    wide = vmem((ROWS, E), F32)
    index = vmem((8, ROWS), jnp.int32)
    owns = [own for _, own, _ in PARTS]
    return [
        wide, vmem((ROWS, FT), BF16), vmem((FT, E), BF16), block, block, wide, vmem((ROWS, 128), F32), vmem((FT, ROWS), BF16),
        block, block, block, block, index, index, index, vmem((ROWS, 128), jnp.int32),
        vmem((ROWS, ROWS), BF16), wide, wide, block, vmem((FT, HALF), BF16), vmem((FT, HALF), BF16), vmem((FT, HALF), BF16),
        *[vmem((3, 4 * own, HALF), BF16) for own in owns],
        *[vmem((4 * own, HALF), BF16) for own in owns],
        *[vmem((3, own, HALF), BF16) for own in owns],
        *[vmem((own, HALF), BF16) for own in owns],
        *[vmem((3, own, 128), BF16) for own in owns],
        dma((SENDS + 2,)),
        *[dma((SENDS,)) for _ in range(10)],
        dma, dma, dma, dma,
        dma((3,)), dma((3,)), dma((3, 3, 3)), dma((3, 3, 3)), dma((3, 3, 3)), dma((3, 3, 3)), dma((3, 4)), dma((3, 4)),
    ]


def on_device(
    picture_embedding_unscaled,
    caption_tower_outputs,
    caption_mapping_matrix,
    matching_caption_index,
    similarity_scaling,
    score_offset,
):
    smem = pl.BlockSpec(memory_space=pltpu.SMEM)
    vmem = pl.BlockSpec(memory_space=pltpu.VMEM)
    anywhere = pl.BlockSpec(memory_space=pl.ANY)
    grad_image, grad_proj = pl.pallas_call(
        kernel,
        out_shape=(jax.ShapeDtypeStruct((ROWS, E), BF16), jax.ShapeDtypeStruct((FT, E), BF16)),
        in_specs=[smem, smem, vmem, anywhere, anywhere, anywhere],
        out_specs=(vmem, vmem),
        scratch_shapes=scratch(),
        compiler_params=pltpu.CompilerParams(
            collective_id=0, has_side_effects=True, vmem_limit_bytes=52 * 1024 * 1024
        ),
    )(
        similarity_scaling, score_offset, matching_caption_index.reshape(1, ROWS),
        picture_embedding_unscaled, caption_tower_outputs, caption_mapping_matrix,
    )
    return grad_image.astype(F32), grad_proj.astype(F32)


def solution(mesh):
    return jax.shard_map(
        on_device,
        mesh=mesh,
        in_specs=(
            P(("group", "blk"), None),
            P(("group", "blk"), None),
            P(),
            P(("group", "blk")),
            P(),
            P(),
        ),
        out_specs=(P(("group", "blk"), None), P()),
        check_vma=False,
    )
```

```python
import jax
import jax.numpy as jnp
from jax import lax
from jax.experimental import pallas as pl
from jax.experimental.pallas import tpu as pltpu
from jax.sharding import PartitionSpec as P

EPS = 1e-06
ROWS = 768
E = 1024
FT = 1280
SEND = 128
SENDS = ROWS // SEND
TILE = 256
TILES = ROWS // TILE
HALF = E // 2
MESH = pl.DeviceIdType.MESH
BF16 = jnp.bfloat16
F32 = jnp.float32

PARTS = ((0, 32, "yzx"), (512, 32, "zyx"), (1024, 16, "xyz"))


def start_copy(src, dst, send, recv, device):
    pltpu.make_async_remote_copy(
        src_ref=src, dst_ref=dst, send_sem=send, recv_sem=recv, device_id=device, device_id_type=MESH
    ).start()


def wait_sent(src, send):
    pltpu.make_async_copy(src, src, send).wait()


def wait_got(dst, recv):
    pltpu.make_async_copy(dst, dst, recv).wait()


def kernel(
    scale_hbm, bias_hbm, index_hbm, pic_hbm, cap_hbm, head_hbm,
    gi_ref, out_ref,
    scale_ref, bias_ref, index_ref, pic, cap, head, iu, tu, tu32, trs, cap_t, images, t2, t3, idx, far_idx, idx_col,
    w, g_text, g_image, gp, hs, r0, d, r1a, r1b, r1c, e_a, e_b, e_c, r2a, r2b, r2c, f_a, f_b, f_c, r3a, r3b, r3c,
    load_sem, is2, is3, is3r, images_got, ts2, tr2, ts3, tr3, ts3r, xs2, xs3, far_idx_got,
    s0s, s0r, rs_s, rs_r, ag_s, ag_r, a0s, a0r,
):
    g = lax.axis_index("group")
    k = lax.axis_index("blk")
    z = g % 4
    y = k // 4
    x = (g // 4) * 2 + (k // 2) % 2
    core = k % 2
    odd = core == 1
    even = core == 0
    place = {"x": x, "y": y, "z": z}

    def device(xx, yy, zz, cc):
        return ((xx // 2) * 4 + zz, yy * 4 + (xx % 2) * 2 + cc)

    def on_axis(axis, d):
        p = dict(place)
        p[axis] = (p[axis] + d) % 4
        return device(p["x"], p["y"], p["z"], core)

    def shift(dg, dk):
        return ((g + dg + 8) % 8, (k + dk + 16) % 16)

    other_core = device(x, y, z, 1 - core)

    loads = []
    for c in range(SENDS):
        loads.append(pltpu.make_async_copy(pic_hbm.at[pl.ds(c * SEND, SEND)], pic.at[pl.ds(c * SEND, SEND)], load_sem.at[c]))
    loads.append(pltpu.make_async_copy(cap_hbm, cap, load_sem.at[SENDS]))
    loads.append(pltpu.make_async_copy(head_hbm, head, load_sem.at[SENDS + 1]))
    loads.append(pltpu.make_async_copy(index_hbm, index_ref, load_sem.at[SENDS + 2]))
    loads.append(pltpu.make_async_copy(scale_hbm, scale_ref, load_sem.at[SENDS + 3]))
    loads.append(pltpu.make_async_copy(bias_hbm, bias_ref, load_sem.at[SENDS + 4]))
    for load in loads:
        load.start()

    barrier = pltpu.get_barrier_semaphore()
    partners = [shift(0, 1), shift(0, -1), shift(1, 0), shift(-1, 0), shift(1, 1), shift(-1, -1), other_core]
    for axis in "xyz":
        for step in (1, 2, 3):
            partners.append(on_axis(axis, step))
    for p in partners:
        pl.semaphore_signal(barrier, inc=1, device_id=p, device_id_type=MESH)

    direct_image = jnp.logical_or(odd, z == 0)
    down = shift(0, -1)
    cross_down = shift(-1, -1)

    def normalize_image(c, _):
        r = pl.ds(pl.multiple_of(c * SEND, SEND), SEND)
        pltpu.make_async_copy(pic.at[r], pic.at[r], load_sem.at[c]).wait()
        v = pic[r, :]
        inv = lax.rsqrt(jnp.sum(v * v, axis=1, keepdims=True) + EPS)
        iu[r, :] = (v * inv).astype(BF16)
        return 0

    def send_image(c, _):
        r = pl.ds(pl.multiple_of(c * SEND, SEND), SEND)
        start_copy(iu.at[r], images.at[0, r], is2.at[c], images_got.at[c], down)

        @pl.when(direct_image)
        def _():
            start_copy(iu.at[r], images.at[1, r], is3.at[c], images_got.at[SENDS + c], cross_down)

        return 0

    def normalize_and_send(c, _):
        normalize_image(c, 0)
        return send_image(c, 0)

    for load in loads[SENDS + 2 :]:
        load.wait()
    scale = scale_ref[0]
    bias = bias_ref[0]
    for c in range(ROWS // 128):
        cols = pl.ds(c * 128, 128)
        square = jnp.broadcast_to(index_ref[cols].reshape(1, 128), (128, 128))
        idx[:, cols] = square[0:8]
        idx_col[cols, :] = square.T
    lax.fori_loop(0, 2, normalize_image, 0)
    pl.semaphore_wait(barrier, len(partners))
    start_copy(idx, far_idx.at[0], xs2, far_idx_got.at[0], down)
    start_copy(idx, far_idx.at[1], xs3, far_idx_got.at[1], cross_down)
    lax.fori_loop(0, 2, send_image, 0)
    lax.fori_loop(2, SENDS, normalize_and_send, 0)

    loads[SENDS].wait()
    loads[SENDS + 1].wait()

    def project(n, _):
        cols = pl.ds(pl.multiple_of(n * TILE, TILE), TILE)
        tu32[:, cols] = jnp.dot(cap[...], head[:, cols], preferred_element_type=F32)
        return 0

    lax.fori_loop(0, E // TILE, project, 0)

    def normalize_text(c, _):
        r = pl.ds(pl.multiple_of(c * SEND, SEND), SEND)
        v = tu32[r, :]
        inv = lax.rsqrt(jnp.sum(v * v, axis=1, keepdims=True) + EPS)
        u = v * inv
        tu32[r, :] = u
        tu[r, :] = u.astype(BF16)
        trs[r, :] = jnp.broadcast_to(inv, (SEND, 128))
        return 0

    lax.fori_loop(0, SENDS, normalize_text, 0)
    up = shift(0, 1)
    cross_up = shift(1, 1)

    def send_t2(first=0, last=SENDS):
        def step(c, _):
            r = pl.ds(pl.multiple_of(c * SEND, SEND), SEND)
            start_copy(tu.at[r], t2.at[r], ts2.at[c], tr2.at[c], up)
            return 0

        lax.fori_loop(first, last, step, 0)

    def send_t3():
        def step(c, _):
            r = pl.ds(pl.multiple_of(c * SEND, SEND), SEND)
            start_copy(tu.at[r], t3.at[r], ts3.at[c], tr3.at[c], cross_up)
            return 0

        lax.fori_loop(0, SENDS, step, 0)

    direct_text = jnp.logical_or(even, z == 3)
    pl.when(even)(send_t2)
    pl.when(jnp.logical_xor(odd, z != 3))(send_t3)

    own_first = (g * 16 + k) * ROWS

    def weights(logits, match):
        v = logits * scale + bias
        v = jnp.where(match, -v, v)
        s = 1.0 / (1.0 + jnp.exp(-v))
        return jnp.where(match, -s, s).astype(BF16)

    def text_logits(c, block, index):
        r = pl.ds(pl.multiple_of(c * TILE, TILE), TILE)
        logits = lax.dot_general(tu[...], block[r, :], (((1,), (1,)), ((), ())), preferred_element_type=F32)
        match = (index[0:1, r] - own_first) == lax.broadcasted_iota(jnp.int32, (ROWS, TILE), 0)
        w[:, r] = weights(logits, match)

    def image_logits(c, texts, first):
        r = pl.ds(pl.multiple_of(c * TILE, TILE), TILE)
        logits = lax.dot_general(iu[...], texts[r, :], (((1,), (1,)), ((), ())), preferred_element_type=F32)
        column = idx_col[...] - (first + c * TILE)
        column = jnp.concatenate([column, column - 128], axis=1)
        match = column == (lax.broadcasted_iota(jnp.int32, (ROWS, TILE), 1) % 128)
        w[:, r] = weights(logits, match)

    def add_grad(total, block, first):
        def step(n, _):
            cols = pl.ds(pl.multiple_of(n * TILE, TILE), TILE)
            term = jnp.dot(w[...], block[:, cols], preferred_element_type=F32)
            total[:, cols] = term if first else total[:, cols] + term
            return 0

        lax.fori_loop(0, E // TILE, step, 0)

    def text_weights(block, index, before):
        def step(c, _):
            before(c)
            text_logits(c, block, index)
            return 0

        lax.fori_loop(0, TILES, step, 0)

    def text_side(block, index, first, before):
        text_weights(block, index, before)
        add_grad(g_text, block, first)

    def image_side(texts, first_row, first, before):
        def step(c, _):
            before(c)
            image_logits(c, texts, first_row)
            return 0

        lax.fori_loop(0, TILES, step, 0)
        add_grad(g_image, texts, first)

    def nothing(c):
        pass

    per = TILE // SEND

    def got(buffer, sems, forward):
        def before(c):
            for i in range(per):
                m = c * per + i
                r = pl.ds(pl.multiple_of(m * SEND, SEND), SEND)
                wait_got(buffer(r), sems(m))
                forward(m, r)

        return before

    def no_forward(m, r):
        pass

    forward_image = jnp.logical_and(odd, z != 0)
    forward_text = jnp.logical_and(even, z != 3)
    forward_early = jnp.logical_and(forward_text, z != 0)
    forward_late = jnp.logical_and(even, z == 0)

    def pass_image(m, r):
        @pl.when(forward_image)
        def _():
            start_copy(images.at[0, r], images.at[1, r], is3r.at[m], images_got.at[SENDS + m], shift(-1, 0))

    def pass_text(c):
        for i in range(per):
            m = c * per + i
            r = pl.ds(pl.multiple_of(m * SEND, SEND), SEND)
            wait_got(t2.at[r], tr2.at[m])
            start_copy(t2.at[r], t3.at[r], ts3r.at[m], tr3.at[m], shift(1, 0))

    first_t2 = (g * 16 + (k + 15) % 16) * ROWS

    def image_t2(before):
        image_side(t2, first_t2, False, before)

    text_side(iu, idx, True, nothing)
    image_side(tu, own_first, True, nothing)

    def turn(n, _):
        cols = pl.ds(pl.multiple_of(n * TILE, TILE), TILE)
        for m in range(TILES):
            cap_t[cols, pl.ds(m * TILE, TILE)] = cap[pl.ds(m * TILE, TILE), cols].T
        return 0

    lax.fori_loop(0, FT // TILE, turn, 0)

    late_row = jnp.logical_and(odd, z == 0)
    one = jnp.where(late_row, 1, 0)
    two = 1 - one
    pl.when(late_row)(lambda: image_t2(got(lambda r: t2.at[r], lambda m: tr2.at[m], no_forward)))

    @pl.when(jnp.logical_and(even, z == 3))
    def _():
        def step(c, _):
            wait_sent(iu.at[pl.ds(pl.multiple_of(c * SEND, SEND), SEND)], is2.at[c])
            return 0

        lax.fori_loop(0, SENDS, step, 0)
        send_t3()

    def before_one(c):
        @pl.when(jnp.logical_and(late_row, c == TILES - 1))
        def _():
            send_t2()

        got(lambda r: images.at[one, r], lambda m: images_got.at[one * SENDS + m], pass_image)(c)

        @pl.when(jnp.logical_and(jnp.logical_and(odd, z != 0), c == TILES - 1))
        def _():
            send_t2()

    wait_got(far_idx.at[one], far_idx_got.at[one])
    text_side(images.at[one], far_idx.at[one], False, before_one)
    pl.when(jnp.logical_and(odd, z != 0))(lambda: image_t2(got(lambda r: t2.at[r], lambda m: tr2.at[m], no_forward)))
    wait_got(far_idx.at[two], far_idx_got.at[two])
    text_weights(images.at[two], far_idx.at[two], got(lambda r: images.at[two, r], lambda m: images_got.at[two * SENDS + m], no_forward))

    def finish_text(c, _):
        r = pl.ds(pl.multiple_of(c * TILE, TILE), TILE)
        u = tu32[r, :]
        v = (g_text[r, :] + jnp.dot(w[r, :], images[two], preferred_element_type=F32)) * scale
        dot = jnp.sum(u * v, axis=1, keepdims=True)
        gp[r, :] = ((v - u * dot) * trs[r, 0:1]).astype(BF16)
        return 0

    lax.fori_loop(0, TILES, finish_text, 0)

    r1 = (r1a, r1b, r1c)
    e_ = (e_a, e_b, e_c)
    r2 = (r2a, r2b, r2c)
    f_ = (f_a, f_b, f_c)
    r3 = (r3a, r3b, r3c)
    mine = pl.multiple_of(core * HALF, HALF)
    theirs = pl.multiple_of((1 - core) * HALF, HALF)

    def span(p):
        base, own, _ = PARTS[p]
        return pl.ds(base, 16 * own)

    for p in range(3):
        rows = span(p)
        for n in range(HALF // TILE):
            hs[rows, pl.ds(n * TILE, TILE)] = jnp.dot(
                cap_t[rows, :], gp[:, pl.ds(pl.multiple_of(theirs + n * TILE, TILE), TILE)], preferred_element_type=F32
            ).astype(BF16)
        start_copy(hs.at[rows], r0.at[rows], s0s.at[p], s0r.at[p], other_core)

    @pl.when(forward_early)
    def _():
        def step(c, _):
            pass_text(c)
            return 0

        lax.fori_loop(0, TILES, step, 0)
        image_t2(nothing)

    @pl.when(forward_late)
    def _():
        def step(c, _):
            pass_text(c)
            return 0

        lax.fori_loop(0, TILES - 1, step, 0)

    for p in range(3):
        base, own, order = PARTS[p]
        rows = span(p)
        for n in range(HALF // TILE):
            term = jnp.dot(
                cap_t[rows, :], gp[:, pl.ds(pl.multiple_of(mine + n * TILE, TILE), TILE)], preferred_element_type=F32
            )
            if n == 0:
                wait_got(r0.at[rows], s0r.at[p])
            cols = pl.ds(n * TILE, TILE)
            d[rows, cols] = (term + r0[rows, cols].astype(F32)).astype(BF16)
        i = place[order[0]]
        for s in (1, 2, 3):
            j = (i + s) % 4
            start_copy(
                d.at[pl.ds(pl.multiple_of(base + j * 4 * own, 16), 4 * own)],
                r1[p].at[s - 1], rs_s.at[p, 0, s - 1], rs_r.at[p, 0, s - 1], on_axis(order[0], s),
            )

    @pl.when(forward_late)
    def _():
        pass_text(TILES - 1)

    def late_t2(c):
        pl.when(z == 3)(lambda: got(lambda r: t2.at[r], lambda m: tr2.at[m], no_forward)(c))

    pl.when(jnp.logical_and(even, jnp.logical_or(z == 0, z == 3)))(lambda: image_t2(late_t2))

    def total(own, parts):
        v = own.astype(F32)
        for s in range(3):
            v = v + parts[s].astype(F32)
        return v.astype(BF16)

    for p in range(3):
        base, own, order = PARTS[p]
        for s in range(3):
            wait_got(r1[p].at[s], rs_r.at[p, 0, s])
        i = place[order[0]]
        e_[p][...] = total(d[pl.ds(pl.multiple_of(base + i * 4 * own, 16), 4 * own), :], [r1[p][s] for s in range(3)])
        i = place[order[1]]
        for s in (1, 2, 3):
            j = (i + s) % 4
            start_copy(
                e_[p].at[pl.ds(pl.multiple_of(j * own, 16), own)],
                r2[p].at[s - 1], rs_s.at[p, 1, s - 1], rs_r.at[p, 1, s - 1], on_axis(order[1], s),
            )
    for p in range(3):
        base, own, order = PARTS[p]
        for s in range(3):
            wait_got(r2[p].at[s], rs_r.at[p, 1, s])
        i = place[order[1]]
        f_[p][...] = total(e_[p][pl.ds(pl.multiple_of(i * own, 16), own), :], [r2[p][s] for s in range(3)])
        i = place[order[2]]
        for s in (1, 2, 3):
            j = (i + s) % 4
            start_copy(
                f_[p].at[:, pl.ds(pl.multiple_of(j * 128, 128), 128)],
                r3[p].at[s - 1], rs_s.at[p, 2, s - 1], rs_r.at[p, 2, s - 1], on_axis(order[2], s),
            )

    def block(p, a, b, c):
        base, own, _ = PARTS[p]
        if a is None:
            rows = pl.ds(base, 16 * own)
        elif b is None:
            rows = pl.ds(pl.multiple_of(base + a * 4 * own, 16), 4 * own)
        else:
            rows = pl.ds(pl.multiple_of(base + (a * 4 + b) * own, 16), own)
        if c is None:
            cols = pl.ds(mine, HALF)
        else:
            cols = pl.ds(pl.multiple_of(mine + c * 128, 128), 128)
        return rows, cols

    def gather(p, stage, rows, cols):
        axis = PARTS[p][2][stage]
        for s in (1, 2, 3):
            ref = out_ref.at[rows, cols]
            start_copy(ref, ref, ag_s.at[p, stage, s - 1], ag_r.at[p, stage, s - 1], on_axis(axis, s))

    def seat(p):
        order = PARTS[p][2]
        return [place[a] for a in order]

    for p in range(3):
        a, b, c = seat(p)
        for s in range(3):
            wait_got(r3[p].at[s], rs_r.at[p, 2, s])
        rows, cols = block(p, a, b, c)
        out_ref[rows, cols] = total(f_[p][:, pl.ds(pl.multiple_of(c * 128, 128), 128)], [r3[p][s] for s in range(3)])
        gather(p, 2, rows, cols)
    for p in range(3):
        a, b, c = seat(p)
        for s in (1, 2, 3):
            wait_got(out_ref.at[block(p, a, b, (c - s + 4) % 4)], ag_r.at[p, 2, s - 1])
        gather(p, 1, *block(p, a, b, None))
    for p in range(3):
        a, b, c = seat(p)
        for s in (1, 2, 3):
            wait_got(out_ref.at[block(p, a, (b - s + 4) % 4, None)], ag_r.at[p, 1, s - 1])
        gather(p, 0, *block(p, a, None, None))
        ref = out_ref.at[block(p, a, None, None)]
        start_copy(ref, ref, a0s.at[p, 0], a0r.at[p, 0], other_core)

    image_side(t3, (((g + 7) % 8) * 16 + (k + 15) % 16) * ROWS, False, got(lambda r: t3.at[r], lambda m: tr3.at[m], no_forward))

    def finish_image(c, _):
        r = pl.ds(pl.multiple_of(c * SEND, SEND), SEND)
        u = pic[r, :]
        inv = lax.rsqrt(jnp.sum(u * u, axis=1, keepdims=True) + EPS)
        u = u * inv
        v = g_image[r, :] * scale
        dot = jnp.sum(u * v, axis=1, keepdims=True)
        gi_ref[r, :] = ((v - u * dot) * inv).astype(BF16)
        return 0

    lax.fori_loop(0, SENDS, finish_image, 0)

    for p in range(3):
        a, b, c = seat(p)
        for s in (1, 2, 3):
            ref = out_ref.at[block(p, (a - s + 4) % 4, None, None)]
            wait_got(ref, ag_r.at[p, 0, s - 1])
            start_copy(ref, ref, a0s.at[p, s], a0r.at[p, s], other_core)
    for p in range(3):
        base, own, _ = PARTS[p]
        a, b, c = seat(p)
        for s in range(4):
            rows = pl.ds(pl.multiple_of(base + ((a - s + 4) % 4) * 4 * own, 16), 4 * own)
            wait_got(out_ref.at[rows, pl.ds(theirs, HALF)], a0r.at[p, s])

    wait_sent(idx, xs2)
    wait_sent(idx, xs3)

    def drain(c, _):
        r = pl.ds(pl.multiple_of(c * SEND, SEND), SEND)
        wait_sent(tu.at[r], ts2.at[c])

        @pl.when(jnp.logical_or(odd, z != 3))
        def _():
            wait_sent(iu.at[r], is2.at[c])

        @pl.when(direct_image)
        def _():
            wait_sent(iu.at[r], is3.at[c])

        @pl.when(direct_text)
        def _():
            wait_sent(tu.at[r], ts3.at[c])

        @pl.when(forward_image)
        def _():
            wait_sent(images.at[0, r], is3r.at[c])

        @pl.when(forward_text)
        def _():
            wait_sent(t2.at[r], ts3r.at[c])

        return 0

    lax.fori_loop(0, SENDS, drain, 0)
    for p in range(3):
        base, own, _ = PARTS[p]
        a, b, c = seat(p)
        wait_sent(hs.at[span(p)], s0s.at[p])
        for s in range(3):
            wait_sent(r1[p].at[s], rs_s.at[p, 0, s])
            wait_sent(r2[p].at[s], rs_s.at[p, 1, s])
            wait_sent(r3[p].at[s], rs_s.at[p, 2, s])
            wait_sent(out_ref.at[block(p, a, b, c)], ag_s.at[p, 2, s])
            wait_sent(out_ref.at[block(p, a, b, None)], ag_s.at[p, 1, s])
            wait_sent(out_ref.at[block(p, a, None, None)], ag_s.at[p, 0, s])
        for s in range(4):
            wait_sent(out_ref.at[block(p, (a - s + 4) % 4, None, None)], a0s.at[p, s])


def scratch():
    vmem = pltpu.VMEM
    dma = pltpu.SemaphoreType.DMA
    block = vmem((ROWS, E), BF16)
    wide = vmem((ROWS, E), F32)
    index = vmem((8, ROWS), jnp.int32)
    owns = [own for _, own, _ in PARTS]
    return [
        pltpu.SMEM((1,), F32), pltpu.SMEM((1,), F32), vmem((ROWS,), jnp.int32), wide, vmem((ROWS, FT), BF16), vmem((FT, E), BF16), block, block, wide, vmem((ROWS, 128), F32), vmem((FT, ROWS), BF16),
        vmem((2, ROWS, E), BF16), block, block, index, vmem((2, 8, ROWS), jnp.int32), vmem((ROWS, 128), jnp.int32),
        vmem((ROWS, ROWS), BF16), wide, wide, block, vmem((FT, HALF), BF16), vmem((FT, HALF), BF16), vmem((FT, HALF), BF16),
        *[vmem((3, 4 * own, HALF), BF16) for own in owns],
        *[vmem((4 * own, HALF), BF16) for own in owns],
        *[vmem((3, own, HALF), BF16) for own in owns],
        *[vmem((own, HALF), BF16) for own in owns],
        *[vmem((3, own, 128), BF16) for own in owns],
        dma((SENDS + 5,)),
        *[dma((SENDS,)) for _ in range(3)], dma((2 * SENDS,)), *[dma((SENDS,)) for _ in range(5)],
        dma, dma, dma((2,)),
        dma((3,)), dma((3,)), dma((3, 3, 3)), dma((3, 3, 3)), dma((3, 3, 3)), dma((3, 3, 3)), dma((3, 4)), dma((3, 4)),
    ]


def widen(a_ref, b_ref, a_out, b_out, a_wide, b_wide, sem):
    copies = []
    for ref, out, wide, first in ((b_ref, b_out, b_wide, 0), (a_ref, a_out, a_wide, FT // TILE)):
        for c in range(ref.shape[0] // TILE):
            r = pl.ds(c * TILE, TILE)
            wide[r, :] = ref[r, :].astype(F32)
            copies.append(pltpu.make_async_copy(wide.at[r], out.at[r], sem.at[first + c]))
            copies[-1].start()
    for copy in copies:
        copy.wait()


def on_device(
    picture_embedding_unscaled,
    caption_tower_outputs,
    caption_mapping_matrix,
    matching_caption_index,
    similarity_scaling,
    score_offset,
):
    vmem = pl.BlockSpec(memory_space=pltpu.VMEM)
    anywhere = pl.BlockSpec(memory_space=pl.ANY)
    grad_image, grad_proj = pl.pallas_call(
        kernel,
        out_shape=(jax.ShapeDtypeStruct((ROWS, E), BF16), jax.ShapeDtypeStruct((FT, E), BF16)),
        in_specs=[pl.BlockSpec(memory_space=pltpu.HBM)] * 6,
        out_specs=(vmem, vmem),
        scratch_shapes=scratch(),
        compiler_params=pltpu.CompilerParams(
            collective_id=0, has_side_effects=True, vmem_limit_bytes=48 * 1024 * 1024
        ),
    )(
        similarity_scaling, score_offset, matching_caption_index,
        picture_embedding_unscaled, caption_tower_outputs, caption_mapping_matrix,
    )
    return pl.pallas_call(
        widen,
        out_shape=(jax.ShapeDtypeStruct((ROWS, E), F32), jax.ShapeDtypeStruct((FT, E), F32)),
        in_specs=[vmem, vmem],
        out_specs=(anywhere, anywhere),
        scratch_shapes=[
            pltpu.VMEM((ROWS, E), F32), pltpu.VMEM((FT, E), F32), pltpu.SemaphoreType.DMA(((ROWS + FT) // TILE,)),
        ],
        compiler_params=pltpu.CompilerParams(vmem_limit_bytes=16 * 1024 * 1024),
    )(grad_image, grad_proj)


def solution(mesh):
    return jax.shard_map(
        on_device,
        mesh=mesh,
        in_specs=(
            P(("group", "blk"), None),
            P(("group", "blk"), None),
            P(),
            P(("group", "blk")),
            P(),
            P(),
        ),
        out_specs=(P(("group", "blk"), None), P()),
        check_vma=False,
    )
```

```python
import jax
import jax.numpy as jnp
from jax import lax
from jax.experimental import pallas as pl
from jax.experimental.pallas import tpu as pltpu
from jax.sharding import PartitionSpec as P

EPS = 1e-06
ROWS = 768
E = 1024
FT = 1280
SEND = 128
SENDS = ROWS // SEND
TILE = 256
TILES = ROWS // TILE
LAST = ROWS - TILE
HALF = E // 2
DETOUR = 2
MESH = pl.DeviceIdType.MESH
BF16 = jnp.bfloat16
F32 = jnp.float32

PARTS = ((0, 32, "zyx"), (512, 32, "yzx"), (1024, 16, "xyz"))


def start_copy(src, dst, send, recv, device):
    pltpu.make_async_remote_copy(
        src_ref=src, dst_ref=dst, send_sem=send, recv_sem=recv, device_id=device, device_id_type=MESH
    ).start()


def wait_sent(src, send):
    pltpu.make_async_copy(src, src, send).wait()


def wait_got(dst, recv):
    pltpu.make_async_copy(dst, dst, recv).wait()


def kernel(
    scale_hbm, bias_hbm, index_hbm, pic_hbm, cap_hbm, head_hbm,
    gi_ref, out_ref,
    scale_ref, bias_ref, index_ref, pic, cap, head, iu, tu, tu32, trs, cap_t, images, t2, t3, tx, idx, far_idx, idx_col,
    w, g_text, g_image, gp, hs, r0, d, r1a, r1b, r1c, e_a, e_b, e_c, r2a, r2b, r2c, f_a, f_b, f_c, r3a, r3b, r3c,
    load_sem, is2, is3, is3r, images_got, ts2, tr2, ts3, tr3, ts3r, txs, txr, txf, xs2, xs3, far_idx_got,
    s0s, s0r, rs_s, rs_r, ag_s, ag_r, a0s, a0r,
):
    g = lax.axis_index("group")
    k = lax.axis_index("blk")
    z = g % 4
    y = k // 4
    x = (g // 4) * 2 + (k // 2) % 2
    core = k % 2
    odd = core == 1
    even = core == 0
    place = {"x": x, "y": y, "z": z}

    def device(xx, yy, zz, cc):
        return ((xx // 2) * 4 + zz, yy * 4 + (xx % 2) * 2 + cc)

    def on_axis(axis, d):
        p = dict(place)
        p[axis] = (p[axis] + d) % 4
        return device(p["x"], p["y"], p["z"], core)

    def shift(dg, dk):
        return ((g + dg + 8) % 8, (k + dk + 16) % 16)

    other_core = device(x, y, z, 1 - core)

    loads = []
    for c in range(SENDS):
        loads.append(pltpu.make_async_copy(pic_hbm.at[pl.ds(c * SEND, SEND)], pic.at[pl.ds(c * SEND, SEND)], load_sem.at[c]))
    loads.append(pltpu.make_async_copy(cap_hbm, cap, load_sem.at[SENDS]))
    loads.append(pltpu.make_async_copy(head_hbm, head, load_sem.at[SENDS + 1]))
    loads.append(pltpu.make_async_copy(index_hbm, index_ref, load_sem.at[SENDS + 2]))
    loads.append(pltpu.make_async_copy(scale_hbm, scale_ref, load_sem.at[SENDS + 3]))
    loads.append(pltpu.make_async_copy(bias_hbm, bias_ref, load_sem.at[SENDS + 4]))
    for load in loads:
        load.start()

    barrier = pltpu.get_barrier_semaphore()
    partners = [shift(0, 1), shift(0, -1), shift(1, 0), shift(-1, 0), shift(1, 1), shift(-1, -1), other_core]
    for axis in "xyz":
        for step in (1, 2, 3):
            partners.append(on_axis(axis, step))
    for p in partners:
        pl.semaphore_signal(barrier, inc=1, device_id=p, device_id_type=MESH)

    direct_image = jnp.logical_or(odd, z == 0)
    late_row = jnp.logical_and(odd, z == 0)
    hand_on = jnp.logical_and(odd, z == 1)
    down = shift(0, -1)
    cross_down = shift(-1, -1)

    def normalize_image(c, _):
        r = pl.ds(pl.multiple_of(c * SEND, SEND), SEND)
        pltpu.make_async_copy(pic.at[r], pic.at[r], load_sem.at[c]).wait()
        v = pic[r, :]
        inv = lax.rsqrt(jnp.sum(v * v, axis=1, keepdims=True) + EPS)
        iu[r, :] = (v * inv).astype(BF16)
        return 0

    def send_image(c, _):
        r = pl.ds(pl.multiple_of(c * SEND, SEND), SEND)
        start_copy(iu.at[r], images.at[0, r], is2.at[c], images_got.at[c], down)

        @pl.when(direct_image)
        def _():
            start_copy(iu.at[r], images.at[1, r], is3.at[c], images_got.at[SENDS + c], cross_down)

        return 0

    def normalize_and_send(c, _):
        normalize_image(c, 0)
        return send_image(c, 0)

    for load in loads[SENDS + 2 :]:
        load.wait()
    scale = scale_ref[0]
    bias = bias_ref[0]
    for c in range(ROWS // 128):
        cols = pl.ds(c * 128, 128)
        square = jnp.broadcast_to(index_ref[cols].reshape(1, 128), (128, 128))
        idx[:, cols] = square[0:8]
        idx_col[cols, :] = square.T
    lax.fori_loop(0, 2, normalize_image, 0)
    pl.semaphore_wait(barrier, len(partners))
    start_copy(idx, far_idx.at[0], xs2, far_idx_got.at[0], down)
    start_copy(idx, far_idx.at[1], xs3, far_idx_got.at[1], cross_down)
    lax.fori_loop(0, 2, send_image, 0)
    lax.fori_loop(2, SENDS, normalize_and_send, 0)

    loads[SENDS].wait()
    loads[SENDS + 1].wait()

    def project(n, _):
        cols = pl.ds(pl.multiple_of(n * TILE, TILE), TILE)
        tu32[:, cols] = jnp.dot(cap[...], head[:, cols], preferred_element_type=F32)
        return 0

    lax.fori_loop(0, E // TILE, project, 0)

    def normalize_text(c, _):
        r = pl.ds(pl.multiple_of(c * SEND, SEND), SEND)
        v = tu32[r, :]
        inv = lax.rsqrt(jnp.sum(v * v, axis=1, keepdims=True) + EPS)
        u = v * inv
        tu32[r, :] = u
        tu[r, :] = u.astype(BF16)
        trs[r, :] = jnp.broadcast_to(inv, (SEND, 128))
        return 0

    lax.fori_loop(0, SENDS, normalize_text, 0)
    up = shift(0, 1)
    cross_up = shift(1, 1)

    def send_t2(first=0, last=SENDS):
        def step(c, _):
            r = pl.ds(pl.multiple_of(c * SEND, SEND), SEND)
            start_copy(tu.at[r], t2.at[r], ts2.at[c], tr2.at[c], up)
            return 0

        lax.fori_loop(first, last, step, 0)

    def send_t3():
        def step(c, _):
            r = pl.ds(pl.multiple_of(c * SEND, SEND), SEND)
            start_copy(tu.at[r], t3.at[r], ts3.at[c], tr3.at[c], cross_up)
            return 0

        lax.fori_loop(0, SENDS, step, 0)

    direct_text = jnp.logical_or(even, z == 3)
    pl.when(even)(send_t2)
    pl.when(jnp.logical_xor(odd, z != 3))(send_t3)

    @pl.when(late_row)
    def _():
        def step(c, _):
            r = pl.ds(pl.multiple_of(c * SEND, SEND), SEND)
            start_copy(tu.at[r], tx.at[r], txs.at[c], txr.at[c], shift(1, 0))
            return 0

        lax.fori_loop(0, DETOUR * (TILE // SEND), step, 0)

    own_first = (g * 16 + k) * ROWS

    def weights(logits, match):
        v = logits * scale + bias
        v = jnp.where(match, -v, v)
        s = 1.0 / (1.0 + jnp.exp(-v))
        return jnp.where(match, -s, s).astype(BF16)

    def text_logits(c, block, index):
        r = pl.ds(pl.multiple_of(c * TILE, TILE), TILE)
        logits = lax.dot_general(tu[...], block[r, :], (((1,), (1,)), ((), ())), preferred_element_type=F32)
        match = (index[0:1, r] - own_first) == lax.broadcasted_iota(jnp.int32, (ROWS, TILE), 0)
        w[:, r] = weights(logits, match)

    def image_logits(c, texts, first):
        r = pl.ds(pl.multiple_of(c * TILE, TILE), TILE)
        logits = lax.dot_general(iu[...], texts[r, :], (((1,), (1,)), ((), ())), preferred_element_type=F32)
        column = idx_col[...] - (first + c * TILE)
        column = jnp.concatenate([column, column - 128], axis=1)
        match = column == (lax.broadcasted_iota(jnp.int32, (ROWS, TILE), 1) % 128)
        w[:, r] = weights(logits, match)

    def add_grad(total, block, first):
        def step(n, _):
            cols = pl.ds(pl.multiple_of(n * TILE, TILE), TILE)
            term = jnp.dot(w[...], block[:, cols], preferred_element_type=F32)
            total[:, cols] = term if first else total[:, cols] + term
            return 0

        lax.fori_loop(0, E // TILE, step, 0)

    def text_weights(block, index, before):
        def step(c, _):
            before(c)
            text_logits(c, block, index)
            return 0

        lax.fori_loop(0, TILES, step, 0)

    def text_side(block, index, first, before):
        text_weights(block, index, before)
        add_grad(g_text, block, first)

    def image_side(texts, first_row, first, before):
        def step(c, _):
            before(c)
            image_logits(c, texts, first_row)
            return 0

        lax.fori_loop(0, TILES, step, 0)
        add_grad(g_image, texts, first)

    def nothing(c):
        pass

    per = TILE // SEND

    def got(buffer, sems, forward):
        def before(c):
            for i in range(per):
                m = c * per + i
                r = pl.ds(pl.multiple_of(m * SEND, SEND), SEND)
                wait_got(buffer(r), sems(m))
                forward(m, r)

        return before

    def no_forward(m, r):
        pass

    forward_image = jnp.logical_and(odd, z != 0)
    forward_text = jnp.logical_and(even, jnp.logical_and(z != 0, z != 3))

    def pass_image(m, r):
        @pl.when(forward_image)
        def _():
            start_copy(images.at[0, r], images.at[1, r], is3r.at[m], images_got.at[SENDS + m], shift(-1, 0))

    def pass_text(c):
        for i in range(per):
            m = c * per + i
            r = pl.ds(pl.multiple_of(m * SEND, SEND), SEND)
            wait_got(t2.at[r], tr2.at[m])
            start_copy(t2.at[r], t3.at[r], ts3r.at[m], tr3.at[m], shift(1, 0))

    first_t2 = (g * 16 + (k + 15) % 16) * ROWS

    def image_t2(before):
        image_side(t2, first_t2, False, before)

    text_side(iu, idx, True, nothing)
    image_side(tu, own_first, True, nothing)

    def turn(n, _):
        cols = pl.ds(pl.multiple_of(n * TILE, TILE), TILE)
        for m in range(TILES):
            cap_t[cols, pl.ds(m * TILE, TILE)] = cap[pl.ds(m * TILE, TILE), cols].T
        return 0

    lax.fori_loop(0, FT // TILE, turn, 0)

    one = jnp.where(late_row, 1, 0)
    two = 1 - one
    pl.when(late_row)(lambda: image_t2(got(lambda r: t2.at[r], lambda m: tr2.at[m], no_forward)))

    @pl.when(jnp.logical_and(even, z == 3))
    def _():
        def step(c, _):
            wait_sent(iu.at[pl.ds(pl.multiple_of(c * SEND, SEND), SEND)], is2.at[c])
            return 0

        lax.fori_loop(0, SENDS, step, 0)
        send_t3()

    def before_one(c):
        @pl.when(jnp.logical_and(late_row, c == 1))
        def _():
            send_t2(DETOUR * per)

        got(lambda r: images.at[one, r], lambda m: images_got.at[one * SENDS + m], pass_image)(c)

        @pl.when(jnp.logical_and(jnp.logical_and(odd, z != 0), c == TILES - 1))
        def _():
            send_t2()

    wait_got(far_idx.at[one], far_idx_got.at[one])
    text_side(images.at[one], far_idx.at[one], False, before_one)
    pl.when(jnp.logical_and(odd, z != 0))(lambda: image_t2(got(lambda r: t2.at[r], lambda m: tr2.at[m], no_forward)))
    wait_got(far_idx.at[two], far_idx_got.at[two])

    def before_two(c):
        got(lambda r: images.at[two, r], lambda m: images_got.at[two * SENDS + m], no_forward)(c)

        @pl.when(jnp.logical_and(hand_on, c < DETOUR))
        def _():
            for i in range(per):
                m = c * per + i
                r = pl.ds(pl.multiple_of(m * SEND, SEND), SEND)
                wait_got(tx.at[r], txr.at[m])
                start_copy(tx.at[r], t3.at[r], txf.at[m], tr3.at[m], shift(0, 1))

    def step_two(c, _):
        before_two(c)
        text_logits(c, images.at[two], far_idx.at[two])

        @pl.when(c == TILES - 2)
        def _():
            def add(n, _):
                cols = pl.ds(pl.multiple_of(n * TILE, TILE), TILE)
                g_text[:, cols] += jnp.dot(w[:, 0:LAST], images[two, 0:LAST, cols], preferred_element_type=F32)
                return 0

            lax.fori_loop(0, E // TILE, add, 0)

        return 0

    lax.fori_loop(0, TILES, step_two, 0)

    def finish_text(c, _):
        r = pl.ds(pl.multiple_of(c * TILE, TILE), TILE)
        u = tu32[r, :]
        v = (g_text[r, :] + jnp.dot(w[r, LAST:], images[two, LAST:], preferred_element_type=F32)) * scale
        dot = jnp.sum(u * v, axis=1, keepdims=True)
        gp[r, :] = ((v - u * dot) * trs[r, 0:1]).astype(BF16)
        return 0

    lax.fori_loop(0, TILES, finish_text, 0)

    r1 = (r1a, r1b, r1c)
    e_ = (e_a, e_b, e_c)
    r2 = (r2a, r2b, r2c)
    f_ = (f_a, f_b, f_c)
    r3 = (r3a, r3b, r3c)
    mine = pl.multiple_of(core * HALF, HALF)
    theirs = pl.multiple_of((1 - core) * HALF, HALF)

    def span(p):
        base, own, _ = PARTS[p]
        return pl.ds(base, 16 * own)

    for p in range(3):
        rows = span(p)
        for n in range(HALF // TILE):
            hs[rows, pl.ds(n * TILE, TILE)] = jnp.dot(
                cap_t[rows, :], gp[:, pl.ds(pl.multiple_of(theirs + n * TILE, TILE), TILE)], preferred_element_type=F32
            ).astype(BF16)
        start_copy(hs.at[rows], r0.at[rows], s0s.at[p], s0r.at[p], other_core)

    @pl.when(forward_text)
    def _():
        def step(c, _):
            pass_text(c)
            return 0

        lax.fori_loop(0, TILES, step, 0)

    first_even = jnp.logical_and(even, z == 0)

    @pl.when(first_even)
    def _():
        for c in range(DETOUR, TILES):
            pass_text(c)

    for p in range(3):
        base, own, order = PARTS[p]
        rows = span(p)
        for n in range(HALF // TILE):
            term = jnp.dot(
                cap_t[rows, :], gp[:, pl.ds(pl.multiple_of(mine + n * TILE, TILE), TILE)], preferred_element_type=F32
            )
            if n == 0:
                wait_got(r0.at[rows], s0r.at[p])
            cols = pl.ds(n * TILE, TILE)
            d[rows, cols] = (term + r0[rows, cols].astype(F32)).astype(BF16)
        i = place[order[0]]
        for s in (1, 2, 3):
            j = (i + s) % 4
            start_copy(
                d.at[pl.ds(pl.multiple_of(base + j * 4 * own, 16), 4 * own)],
                r1[p].at[s - 1], rs_s.at[p, 0, s - 1], rs_r.at[p, 0, s - 1], on_axis(order[0], s),
            )

    def late_t2(c):
        pl.when(jnp.logical_not(forward_text))(lambda: got(lambda r: t2.at[r], lambda m: tr2.at[m], no_forward)(c))

    hand_down = jnp.logical_and(even, z == 1)

    @pl.when(hand_down)
    def _():
        def step(m, _):
            r = pl.ds(pl.multiple_of(m * SEND, SEND), SEND)
            wait_got(t3.at[r], tr3.at[m])
            start_copy(t3.at[r], t2.at[r], txf.at[m], tr2.at[m], shift(-1, 0))
            return 0

        lax.fori_loop(0, DETOUR * per, step, 0)

    pl.when(jnp.logical_and(even, z != 0))(lambda: image_t2(late_t2))

    @pl.when(first_even)
    def _():
        for c in range(DETOUR, TILES):
            image_logits(c, t2, first_t2)

    def total(own, parts):
        v = own.astype(F32)
        for s in range(3):
            v = v + parts[s].astype(F32)
        return v.astype(BF16)

    for p in range(3):
        base, own, order = PARTS[p]
        for s in range(3):
            wait_got(r1[p].at[s], rs_r.at[p, 0, s])
        i = place[order[0]]
        e_[p][...] = total(d[pl.ds(pl.multiple_of(base + i * 4 * own, 16), 4 * own), :], [r1[p][s] for s in range(3)])
        i = place[order[1]]
        for s in (1, 2, 3):
            j = (i + s) % 4
            start_copy(
                e_[p].at[pl.ds(pl.multiple_of(j * own, 16), own)],
                r2[p].at[s - 1], rs_s.at[p, 1, s - 1], rs_r.at[p, 1, s - 1], on_axis(order[1], s),
            )

    @pl.when(first_even)
    def _():
        def step(c, _):
            got(lambda r: t2.at[r], lambda m: tr2.at[m], no_forward)(c)
            image_logits(c, t2, first_t2)
            return 0

        lax.fori_loop(0, DETOUR, step, 0)

    for p in range(3):
        base, own, order = PARTS[p]
        for s in range(3):
            wait_got(r2[p].at[s], rs_r.at[p, 1, s])
        i = place[order[1]]
        f_[p][...] = total(e_[p][pl.ds(pl.multiple_of(i * own, 16), own), :], [r2[p][s] for s in range(3)])
        i = place[order[2]]
        for s in (1, 2, 3):
            j = (i + s) % 4
            start_copy(
                f_[p].at[:, pl.ds(pl.multiple_of(j * 128, 128), 128)],
                r3[p].at[s - 1], rs_s.at[p, 2, s - 1], rs_r.at[p, 2, s - 1], on_axis(order[2], s),
            )

    def image_t3(c):
        if c < DETOUR:
            pl.when(jnp.logical_not(hand_down))(lambda: got(lambda r: t3.at[r], lambda m: tr3.at[m], no_forward)(c))
        else:
            got(lambda r: t3.at[r], lambda m: tr3.at[m], no_forward)(c)
        image_logits(c, t3, (((g + 7) % 8) * 16 + (k + 15) % 16) * ROWS)

    pl.when(first_even)(lambda: add_grad(g_image, t2, False))
    pl.when(jnp.logical_not(first_even))(lambda: image_t3(0))

    def block(p, a, b, c):
        base, own, _ = PARTS[p]
        if a is None:
            rows = pl.ds(base, 16 * own)
        elif b is None:
            rows = pl.ds(pl.multiple_of(base + a * 4 * own, 16), 4 * own)
        else:
            rows = pl.ds(pl.multiple_of(base + (a * 4 + b) * own, 16), own)
        if c is None:
            cols = pl.ds(mine, HALF)
        else:
            cols = pl.ds(pl.multiple_of(mine + c * 128, 128), 128)
        return rows, cols

    def gather(p, stage, rows, cols):
        axis = PARTS[p][2][stage]
        for s in (1, 2, 3):
            ref = out_ref.at[rows, cols]
            start_copy(ref, ref, ag_s.at[p, stage, s - 1], ag_r.at[p, stage, s - 1], on_axis(axis, s))

    def seat(p):
        order = PARTS[p][2]
        return [place[a] for a in order]

    for p in range(3):
        a, b, c = seat(p)
        for s in range(3):
            wait_got(r3[p].at[s], rs_r.at[p, 2, s])
        rows, cols = block(p, a, b, c)
        out_ref[rows, cols] = total(f_[p][:, pl.ds(pl.multiple_of(c * 128, 128), 128)], [r3[p][s] for s in range(3)])
        gather(p, 2, rows, cols)
    pl.when(first_even)(lambda: image_t3(0))
    image_t3(1)
    for p in range(3):
        a, b, c = seat(p)
        for s in (1, 2, 3):
            wait_got(out_ref.at[block(p, a, b, (c - s + 4) % 4)], ag_r.at[p, 2, s - 1])
        gather(p, 1, *block(p, a, b, None))
    image_t3(2)
    for p in range(3):
        a, b, c = seat(p)
        for s in (1, 2, 3):
            wait_got(out_ref.at[block(p, a, (b - s + 4) % 4, None)], ag_r.at[p, 1, s - 1])
        gather(p, 0, *block(p, a, None, None))
        ref = out_ref.at[block(p, a, None, None)]
        start_copy(ref, ref, a0s.at[p, 0], a0r.at[p, 0], other_core)

    add_grad(g_image, t3, False)

    def finish_image(c, _):
        r = pl.ds(pl.multiple_of(c * SEND, SEND), SEND)
        u = pic[r, :]
        inv = lax.rsqrt(jnp.sum(u * u, axis=1, keepdims=True) + EPS)
        u = u * inv
        v = g_image[r, :] * scale
        dot = jnp.sum(u * v, axis=1, keepdims=True)
        gi_ref[r, :] = ((v - u * dot) * inv).astype(BF16)
        return 0

    lax.fori_loop(0, SENDS, finish_image, 0)

    for p in range(3):
        a, b, c = seat(p)
        for s in (1, 2, 3):
            ref = out_ref.at[block(p, (a - s + 4) % 4, None, None)]
            wait_got(ref, ag_r.at[p, 0, s - 1])
            start_copy(ref, ref, a0s.at[p, s], a0r.at[p, s], other_core)
    for p in range(3):
        base, own, _ = PARTS[p]
        a, b, c = seat(p)
        for s in range(4):
            rows = pl.ds(pl.multiple_of(base + ((a - s + 4) % 4) * 4 * own, 16), 4 * own)
            wait_got(out_ref.at[rows, pl.ds(theirs, HALF)], a0r.at[p, s])

    wait_sent(idx, xs2)
    wait_sent(idx, xs3)

    def drain(c, _):
        r = pl.ds(pl.multiple_of(c * SEND, SEND), SEND)
        @pl.when(jnp.logical_not(jnp.logical_and(late_row, c < DETOUR * per)))
        def _():
            wait_sent(tu.at[r], ts2.at[c])

        @pl.when(jnp.logical_or(odd, z != 3))
        def _():
            wait_sent(iu.at[r], is2.at[c])

        @pl.when(direct_image)
        def _():
            wait_sent(iu.at[r], is3.at[c])

        @pl.when(direct_text)
        def _():
            wait_sent(tu.at[r], ts3.at[c])

        @pl.when(forward_image)
        def _():
            wait_sent(images.at[0, r], is3r.at[c])

        @pl.when(jnp.logical_or(forward_text, jnp.logical_and(first_even, c >= DETOUR * per)))
        def _():
            wait_sent(t2.at[r], ts3r.at[c])

        @pl.when(jnp.logical_and(late_row, c < DETOUR * per))
        def _():
            wait_sent(tu.at[r], txs.at[c])

        @pl.when(jnp.logical_and(z == 1, c < DETOUR * per))
        def _():
            wait_sent(tx.at[r], txf.at[c])

        return 0

    lax.fori_loop(0, SENDS, drain, 0)
    for p in range(3):
        base, own, _ = PARTS[p]
        a, b, c = seat(p)
        wait_sent(hs.at[span(p)], s0s.at[p])
        for s in range(3):
            wait_sent(r1[p].at[s], rs_s.at[p, 0, s])
            wait_sent(r2[p].at[s], rs_s.at[p, 1, s])
            wait_sent(r3[p].at[s], rs_s.at[p, 2, s])
            wait_sent(out_ref.at[block(p, a, b, c)], ag_s.at[p, 2, s])
            wait_sent(out_ref.at[block(p, a, b, None)], ag_s.at[p, 1, s])
            wait_sent(out_ref.at[block(p, a, None, None)], ag_s.at[p, 0, s])
        for s in range(4):
            wait_sent(out_ref.at[block(p, (a - s + 4) % 4, None, None)], a0s.at[p, s])


def scratch():
    vmem = pltpu.VMEM
    dma = pltpu.SemaphoreType.DMA
    block = vmem((ROWS, E), BF16)
    wide = vmem((ROWS, E), F32)
    index = vmem((8, ROWS), jnp.int32)
    owns = [own for _, own, _ in PARTS]
    return [
        pltpu.SMEM((1,), F32), pltpu.SMEM((1,), F32), vmem((ROWS,), jnp.int32), wide, vmem((ROWS, FT), BF16), vmem((FT, E), BF16), block, block, wide, vmem((ROWS, 128), F32), vmem((FT, ROWS), BF16),
        vmem((2, ROWS, E), BF16), block, block, block, index, vmem((2, 8, ROWS), jnp.int32), vmem((ROWS, 128), jnp.int32),
        vmem((ROWS, ROWS), BF16), wide, wide, block, vmem((FT, HALF), BF16), vmem((FT, HALF), BF16), vmem((FT, HALF), BF16),
        *[vmem((3, 4 * own, HALF), BF16) for own in owns],
        *[vmem((4 * own, HALF), BF16) for own in owns],
        *[vmem((3, own, HALF), BF16) for own in owns],
        *[vmem((own, HALF), BF16) for own in owns],
        *[vmem((3, own, 128), BF16) for own in owns],
        dma((SENDS + 5,)),
        *[dma((SENDS,)) for _ in range(3)], dma((2 * SENDS,)), *[dma((SENDS,)) for _ in range(8)],
        dma, dma, dma((2,)),
        dma((3,)), dma((3,)), dma((3, 3, 3)), dma((3, 3, 3)), dma((3, 3, 3)), dma((3, 3, 3)), dma((3, 4)), dma((3, 4)),
    ]


def widen(a_ref, b_ref, a_out, b_out, a_wide, b_wide, sem):
    copies = []
    for ref, out, wide, first in ((b_ref, b_out, b_wide, 0), (a_ref, a_out, a_wide, FT // TILE)):
        for c in range(ref.shape[0] // TILE):
            r = pl.ds(c * TILE, TILE)
            wide[r, :] = ref[r, :].astype(F32)
            copies.append(pltpu.make_async_copy(wide.at[r], out.at[r], sem.at[first + c]))
            copies[-1].start()
    for copy in copies:
        copy.wait()


def on_device(
    picture_embedding_unscaled,
    caption_tower_outputs,
    caption_mapping_matrix,
    matching_caption_index,
    similarity_scaling,
    score_offset,
):
    vmem = pl.BlockSpec(memory_space=pltpu.VMEM)
    anywhere = pl.BlockSpec(memory_space=pl.ANY)
    grad_image, grad_proj = pl.pallas_call(
        kernel,
        out_shape=(jax.ShapeDtypeStruct((ROWS, E), BF16), jax.ShapeDtypeStruct((FT, E), BF16)),
        in_specs=[pl.BlockSpec(memory_space=pltpu.HBM)] * 6,
        out_specs=(vmem, vmem),
        scratch_shapes=scratch(),
        compiler_params=pltpu.CompilerParams(
            collective_id=0, has_side_effects=True, vmem_limit_bytes=48 * 1024 * 1024
        ),
    )(
        similarity_scaling, score_offset, matching_caption_index,
        picture_embedding_unscaled, caption_tower_outputs, caption_mapping_matrix,
    )
    return pl.pallas_call(
        widen,
        out_shape=(jax.ShapeDtypeStruct((ROWS, E), F32), jax.ShapeDtypeStruct((FT, E), F32)),
        in_specs=[vmem, vmem],
        out_specs=(anywhere, anywhere),
        scratch_shapes=[
            pltpu.VMEM((ROWS, E), F32), pltpu.VMEM((FT, E), F32), pltpu.SemaphoreType.DMA(((ROWS + FT) // TILE,)),
        ],
        compiler_params=pltpu.CompilerParams(vmem_limit_bytes=16 * 1024 * 1024),
    )(grad_image, grad_proj)


def solution(mesh):
    return jax.shard_map(
        on_device,
        mesh=mesh,
        in_specs=(
            P(("group", "blk"), None),
            P(("group", "blk"), None),
            P(),
            P(("group", "blk")),
            P(),
            P(),
        ),
        out_specs=(P(("group", "blk"), None), P()),
        check_vma=False,
    )
```

```python
import jax
import jax.numpy as jnp
from jax import lax
from jax.experimental import pallas as pl
from jax.experimental.pallas import tpu as pltpu
from jax.sharding import PartitionSpec as P

EPS = 1e-06
ROWS = 768
E = 1024
FT = 1280
SEND = 128
SENDS = ROWS // SEND
TILE = 256
TILES = ROWS // TILE
LAST = ROWS - TILE
HALF = E // 2
DETOUR = 2
DETOUR_BACK = 1
MESH = pl.DeviceIdType.MESH
BF16 = jnp.bfloat16
F32 = jnp.float32

PARTS = ((0, 32, "zyx"), (512, 32, "yzx"), (1024, 16, "xyz"))


def start_copy(src, dst, send, recv, device):
    pltpu.make_async_remote_copy(
        src_ref=src, dst_ref=dst, send_sem=send, recv_sem=recv, device_id=device, device_id_type=MESH
    ).start()


def wait_sent(src, send):
    pltpu.make_async_copy(src, src, send).wait()


def wait_got(dst, recv):
    pltpu.make_async_copy(dst, dst, recv).wait()


def kernel(
    scale_hbm, bias_hbm, index_hbm, pic_hbm, cap_hbm, head_hbm,
    gi_ref, out_ref,
    scale_ref, bias_ref, index_ref, pic, cap, head, iu, tu, tu32, trs, cap_t, images, t2, t3, tx, idx, far_idx, idx_col,
    w, g_text, g_image, gp, hs, r0, d, r1a, r1b, r1c, e_a, e_b, e_c, r2a, r2b, r2c, r3a, r3b, r3c,
    load_sem, is2, is3, is3r, images_got, ts2, tr2, ts3, tr3, ts3r, txs, txr, txf, xs2, xs3, far_idx_got,
    s0s, s0r, rs_s, rs_r, ag_s, ag_r, a0s, a0r,
):
    g = lax.axis_index("group")
    k = lax.axis_index("blk")
    z = g % 4
    y = k // 4
    x = (g // 4) * 2 + (k // 2) % 2
    core = k % 2
    odd = core == 1
    even = core == 0
    place = {"x": x, "y": y, "z": z}

    def device(xx, yy, zz, cc):
        return ((xx // 2) * 4 + zz, yy * 4 + (xx % 2) * 2 + cc)

    def on_axis(axis, d):
        p = dict(place)
        p[axis] = (p[axis] + d) % 4
        return device(p["x"], p["y"], p["z"], core)

    def shift(dg, dk):
        return ((g + dg + 8) % 8, (k + dk + 16) % 16)

    other_core = device(x, y, z, 1 - core)

    loads = []
    for c in range(SENDS):
        loads.append(pltpu.make_async_copy(pic_hbm.at[pl.ds(c * SEND, SEND)], pic.at[pl.ds(c * SEND, SEND)], load_sem.at[c]))
    loads.append(pltpu.make_async_copy(cap_hbm, cap, load_sem.at[SENDS]))
    loads.append(pltpu.make_async_copy(head_hbm, head, load_sem.at[SENDS + 1]))
    loads.append(pltpu.make_async_copy(index_hbm, index_ref, load_sem.at[SENDS + 2]))
    loads.append(pltpu.make_async_copy(scale_hbm, scale_ref, load_sem.at[SENDS + 3]))
    loads.append(pltpu.make_async_copy(bias_hbm, bias_ref, load_sem.at[SENDS + 4]))
    for load in loads:
        load.start()

    barrier = pltpu.get_barrier_semaphore()
    partners = [shift(0, 1), shift(0, -1), shift(1, 0), shift(-1, 0), shift(1, 1), shift(-1, -1), other_core]
    for axis in "xyz":
        for step in (1, 2, 3):
            partners.append(on_axis(axis, step))
    for p in partners:
        pl.semaphore_signal(barrier, inc=1, device_id=p, device_id_type=MESH)

    direct_image = jnp.logical_or(odd, z == 0)
    late_row = jnp.logical_and(odd, z == 0)
    hand_on = jnp.logical_and(odd, z == 1)
    last_odd = jnp.logical_and(odd, z == 3)
    hand_back = jnp.logical_and(odd, z == 2)
    down = shift(0, -1)
    cross_down = shift(-1, -1)

    def normalize_image(c, _):
        r = pl.ds(pl.multiple_of(c * SEND, SEND), SEND)
        pltpu.make_async_copy(pic.at[r], pic.at[r], load_sem.at[c]).wait()
        v = pic[r, :]
        inv = lax.rsqrt(jnp.sum(v * v, axis=1, keepdims=True) + EPS)
        iu[r, :] = (v * inv).astype(BF16)
        return 0

    def send_image(c, _):
        r = pl.ds(pl.multiple_of(c * SEND, SEND), SEND)
        start_copy(iu.at[r], images.at[0, r], is2.at[c], images_got.at[c], down)

        @pl.when(direct_image)
        def _():
            start_copy(iu.at[r], images.at[1, r], is3.at[c], images_got.at[SENDS + c], cross_down)

        return 0

    def normalize_and_send(c, _):
        normalize_image(c, 0)
        return send_image(c, 0)

    for load in loads[SENDS + 2 :]:
        load.wait()
    scale = scale_ref[0]
    bias = bias_ref[0]
    for c in range(ROWS // 128):
        cols = pl.ds(c * 128, 128)
        square = jnp.broadcast_to(index_ref[cols].reshape(1, 128), (128, 128))
        idx[:, cols] = square[0:8]
        idx_col[cols, :] = square.T
    lax.fori_loop(0, 2, normalize_image, 0)
    pl.semaphore_wait(barrier, len(partners))
    start_copy(idx, far_idx.at[0], xs2, far_idx_got.at[0], down)
    start_copy(idx, far_idx.at[1], xs3, far_idx_got.at[1], cross_down)
    lax.fori_loop(0, 2, send_image, 0)
    lax.fori_loop(2, SENDS, normalize_and_send, 0)

    loads[SENDS].wait()
    loads[SENDS + 1].wait()

    def project(n, _):
        cols = pl.ds(pl.multiple_of(n * TILE, TILE), TILE)
        tu32[:, cols] = jnp.dot(cap[...], head[:, cols], preferred_element_type=F32)
        return 0

    lax.fori_loop(0, E // TILE, project, 0)

    def normalize_text(c, _):
        r = pl.ds(pl.multiple_of(c * SEND, SEND), SEND)
        v = tu32[r, :]
        inv = lax.rsqrt(jnp.sum(v * v, axis=1, keepdims=True) + EPS)
        u = v * inv
        tu32[r, :] = u
        tu[r, :] = u.astype(BF16)
        trs[r, :] = jnp.broadcast_to(inv, (SEND, 128))
        return 0

    lax.fori_loop(0, SENDS, normalize_text, 0)
    up = shift(0, 1)
    cross_up = shift(1, 1)

    def send_t2(first=0, last=SENDS):
        def step(c, _):
            r = pl.ds(pl.multiple_of(c * SEND, SEND), SEND)
            start_copy(tu.at[r], t2.at[r], ts2.at[c], tr2.at[c], up)
            return 0

        lax.fori_loop(first, last, step, 0)

    def send_t3():
        def step(c, _):
            r = pl.ds(pl.multiple_of(c * SEND, SEND), SEND)
            start_copy(tu.at[r], t3.at[r], ts3.at[c], tr3.at[c], cross_up)
            return 0

        lax.fori_loop(0, SENDS, step, 0)

    direct_text = jnp.logical_or(even, z == 3)
    pl.when(even)(send_t2)
    pl.when(jnp.logical_xor(odd, z != 3))(send_t3)

    @pl.when(late_row)
    def _():
        def step(c, _):
            r = pl.ds(pl.multiple_of(c * SEND, SEND), SEND)
            start_copy(tu.at[r], tx.at[r], txs.at[c], txr.at[c], shift(1, 0))
            return 0

        lax.fori_loop(0, DETOUR * (TILE // SEND), step, 0)

    own_first = (g * 16 + k) * ROWS

    def weights(logits, match):
        v = logits * scale + bias
        v = jnp.where(match, -v, v)
        s = 1.0 / (1.0 + jnp.exp(-v))
        return jnp.where(match, -s, s).astype(BF16)

    def text_logits(c, block, index):
        r = pl.ds(pl.multiple_of(c * TILE, TILE), TILE)
        logits = lax.dot_general(tu[...], block[r, :], (((1,), (1,)), ((), ())), preferred_element_type=F32)
        match = (index[0:1, r] - own_first) == lax.broadcasted_iota(jnp.int32, (ROWS, TILE), 0)
        w[:, r] = weights(logits, match)

    def image_logits(c, texts, first):
        r = pl.ds(pl.multiple_of(c * TILE, TILE), TILE)
        logits = lax.dot_general(iu[...], texts[r, :], (((1,), (1,)), ((), ())), preferred_element_type=F32)
        column = idx_col[...] - (first + c * TILE)
        column = jnp.concatenate([column, column - 128], axis=1)
        match = column == (lax.broadcasted_iota(jnp.int32, (ROWS, TILE), 1) % 128)
        w[:, r] = weights(logits, match)

    def add_grad(total, block, first):
        def step(n, _):
            cols = pl.ds(pl.multiple_of(n * TILE, TILE), TILE)
            term = jnp.dot(w[...], block[:, cols], preferred_element_type=F32)
            total[:, cols] = term if first else total[:, cols] + term
            return 0

        lax.fori_loop(0, E // TILE, step, 0)

    def text_weights(block, index, before):
        def step(c, _):
            before(c)
            text_logits(c, block, index)
            return 0

        lax.fori_loop(0, TILES, step, 0)

    def text_side(block, index, first, before):
        text_weights(block, index, before)
        add_grad(g_text, block, first)

    def image_side(texts, first_row, first, before):
        def step(c, _):
            before(c)
            image_logits(c, texts, first_row)
            return 0

        lax.fori_loop(0, TILES, step, 0)
        add_grad(g_image, texts, first)

    def nothing(c):
        pass

    per = TILE // SEND

    def got(buffer, sems, forward):
        def before(c):
            for i in range(per):
                m = c * per + i
                r = pl.ds(pl.multiple_of(m * SEND, SEND), SEND)
                wait_got(buffer(r), sems(m))
                forward(m, r)

        return before

    def no_forward(m, r):
        pass

    forward_image = jnp.logical_and(odd, z != 0)
    forward_text = jnp.logical_and(even, jnp.logical_and(z != 0, z != 3))

    def pass_image(m, r):
        @pl.when(forward_image)
        def _():
            start_copy(images.at[0, r], images.at[1, r], is3r.at[m], images_got.at[SENDS + m], shift(-1, 0))

    def pass_text(c):
        for i in range(per):
            m = c * per + i
            r = pl.ds(pl.multiple_of(m * SEND, SEND), SEND)
            wait_got(t2.at[r], tr2.at[m])
            start_copy(t2.at[r], t3.at[r], ts3r.at[m], tr3.at[m], shift(1, 0))

    first_t2 = (g * 16 + (k + 15) % 16) * ROWS

    def image_t2(before):
        image_side(t2, first_t2, False, before)

    text_side(iu, idx, True, nothing)
    image_side(tu, own_first, True, nothing)

    def turn(n, _):
        cols = pl.ds(pl.multiple_of(n * TILE, TILE), TILE)
        for m in range(TILES):
            cap_t[cols, pl.ds(m * TILE, TILE)] = cap[pl.ds(m * TILE, TILE), cols].T
        return 0

    lax.fori_loop(0, FT // TILE, turn, 0)

    one = jnp.where(late_row, 1, 0)
    two = 1 - one
    pl.when(late_row)(lambda: image_t2(got(lambda r: t2.at[r], lambda m: tr2.at[m], no_forward)))

    @pl.when(jnp.logical_and(even, z == 3))
    def _():
        def step(c, _):
            wait_sent(iu.at[pl.ds(pl.multiple_of(c * SEND, SEND), SEND)], is2.at[c])
            return 0

        lax.fori_loop(0, SENDS, step, 0)
        send_t3()

    def before_one(c):
        @pl.when(jnp.logical_and(late_row, c == 1))
        def _():
            send_t2(DETOUR * per)

        got(lambda r: images.at[one, r], lambda m: images_got.at[one * SENDS + m], pass_image)(c)

        @pl.when(jnp.logical_and(jnp.logical_and(odd, jnp.logical_and(z != 0, z != 3)), c == TILES - 1))
        def _():
            send_t2()

        @pl.when(jnp.logical_and(last_odd, c == TILES - 1))
        def _():
            def step(m, _):
                r = pl.ds(pl.multiple_of(m * SEND, SEND), SEND)
                start_copy(tu.at[r], tx.at[r], txs.at[m], txr.at[m], shift(-1, 0))
                return 0

            send_t2(DETOUR_BACK * per)
            lax.fori_loop(0, DETOUR_BACK * per, step, 0)

    wait_got(far_idx.at[one], far_idx_got.at[one])
    text_side(images.at[one], far_idx.at[one], False, before_one)
    pl.when(jnp.logical_and(odd, z != 0))(lambda: image_t2(got(lambda r: t2.at[r], lambda m: tr2.at[m], no_forward)))
    wait_got(far_idx.at[two], far_idx_got.at[two])

    def before_two(c):
        got(lambda r: images.at[two, r], lambda m: images_got.at[two * SENDS + m], no_forward)(c)

        @pl.when(jnp.logical_and(hand_on, c < DETOUR))
        def _():
            for i in range(per):
                m = c * per + i
                r = pl.ds(pl.multiple_of(m * SEND, SEND), SEND)
                wait_got(tx.at[r], txr.at[m])
                start_copy(tx.at[r], t3.at[r], txf.at[m], tr3.at[m], shift(0, 1))

    def step_two(c, _):
        before_two(c)
        text_logits(c, images.at[two], far_idx.at[two])

        @pl.when(c == TILES - 2)
        def _():
            def add(n, _):
                cols = pl.ds(pl.multiple_of(n * TILE, TILE), TILE)
                g_text[:, cols] += jnp.dot(w[:, 0:LAST], images[two, 0:LAST, cols], preferred_element_type=F32)
                return 0

            lax.fori_loop(0, E // TILE, add, 0)

        return 0

    lax.fori_loop(0, TILES, step_two, 0)

    def finish_text(c, _):
        r = pl.ds(pl.multiple_of(c * TILE, TILE), TILE)
        u = tu32[r, :]
        v = (g_text[r, :] + jnp.dot(w[r, LAST:], images[two, LAST:], preferred_element_type=F32)) * scale
        dot = jnp.sum(u * v, axis=1, keepdims=True)
        gp[r, :] = ((v - u * dot) * trs[r, 0:1]).astype(BF16)
        return 0

    lax.fori_loop(0, TILES, finish_text, 0)

    r1 = (r1a, r1b, r1c)
    e_ = (e_a, e_b, e_c)
    r2 = (r2a, r2b, r2c)
    r3 = (r3a, r3b, r3c)
    mine = pl.multiple_of(core * HALF, HALF)
    theirs = pl.multiple_of((1 - core) * HALF, HALF)

    def span(p):
        base, own, _ = PARTS[p]
        return pl.ds(base, 16 * own)

    for p in range(3):
        rows = span(p)
        for n in range(HALF // TILE):
            hs[rows, pl.ds(n * TILE, TILE)] = jnp.dot(
                cap_t[rows, :], gp[:, pl.ds(pl.multiple_of(theirs + n * TILE, TILE), TILE)], preferred_element_type=F32
            ).astype(BF16)
        start_copy(hs.at[rows], r0.at[rows], s0s.at[p], s0r.at[p], other_core)

    @pl.when(forward_text)
    def _():
        def step(c, _):
            pass_text(c)
            return 0

        lax.fori_loop(0, TILES, step, 0)

    first_even = jnp.logical_and(even, z == 0)

    @pl.when(first_even)
    def _():
        for c in range(DETOUR, TILES):
            pass_text(c)

    for p in range(3):
        base, own, order = PARTS[p]
        rows = span(p)
        for n in range(HALF // TILE):
            term = jnp.dot(
                cap_t[rows, :], gp[:, pl.ds(pl.multiple_of(mine + n * TILE, TILE), TILE)], preferred_element_type=F32
            )
            if n == 0:
                wait_got(r0.at[rows], s0r.at[p])
            cols = pl.ds(n * TILE, TILE)
            d[rows, cols] = (term + r0[rows, cols].astype(F32)).astype(BF16)
        i = place[order[0]]
        for s in (1, 2, 3):
            j = (i + s) % 4
            start_copy(
                d.at[pl.ds(pl.multiple_of(base + j * 4 * own, 16), 4 * own)],
                r1[p].at[s - 1], rs_s.at[p, 0, s - 1], rs_r.at[p, 0, s - 1], on_axis(order[0], s),
            )

    mid_even = jnp.logical_and(even, jnp.logical_or(z == 1, z == 2))
    outer_even = jnp.logical_and(even, jnp.logical_or(z == 0, z == 3))
    pl.when(mid_even)(lambda: image_t2(nothing))

    def tile_t2(c):
        got(lambda r: t2.at[r], lambda m: tr2.at[m], no_forward)(c)
        image_logits(c, t2, first_t2)

    @pl.when(outer_even)
    def _():
        def step(c, _):
            pl.when(z == 3)(lambda: got(lambda r: t2.at[r], lambda m: tr2.at[m], no_forward)(c))
            image_logits(c, t2, first_t2)
            return 0

        lax.fori_loop(jnp.where(z == 0, DETOUR, DETOUR_BACK), TILES, step, 0)

    hand_down = jnp.logical_and(even, z == 1)

    @pl.when(hand_down)
    def _():
        def step(m, _):
            r = pl.ds(pl.multiple_of(m * SEND, SEND), SEND)
            wait_got(t3.at[r], tr3.at[m])
            start_copy(t3.at[r], t2.at[r], txf.at[m], tr2.at[m], shift(-1, 0))
            return 0

        lax.fori_loop(0, DETOUR * per, step, 0)

    @pl.when(hand_back)
    def _():
        def step(m, _):
            r = pl.ds(pl.multiple_of(m * SEND, SEND), SEND)
            wait_got(tx.at[r], txr.at[m])
            start_copy(tx.at[r], t2.at[r], txf.at[m], tr2.at[m], shift(1, 1))
            return 0

        lax.fori_loop(0, DETOUR_BACK * per, step, 0)

    def total(own, parts):
        v = own.astype(F32)
        for s in range(3):
            v = v + parts[s].astype(F32)
        return v.astype(BF16)

    for p in range(3):
        base, own, order = PARTS[p]
        for s in range(3):
            wait_got(r1[p].at[s], rs_r.at[p, 0, s])
        i = place[order[0]]
        e_[p][...] = total(d[pl.ds(pl.multiple_of(base + i * 4 * own, 16), 4 * own), :], [r1[p][s] for s in range(3)])
        i = place[order[1]]
        for s in (1, 2, 3):
            j = (i + s) % 4
            start_copy(
                e_[p].at[pl.ds(pl.multiple_of(j * own, 16), own)],
                r2[p].at[s - 1], rs_s.at[p, 1, s - 1], rs_r.at[p, 1, s - 1], on_axis(order[1], s),
            )

    @pl.when(outer_even)
    def _():
        def step(c, _):
            tile_t2(c)
            return 0

        lax.fori_loop(0, jnp.where(z == 0, DETOUR, DETOUR_BACK), step, 0)

    for p in range(3):
        base, own, order = PARTS[p]
        for s in range(3):
            wait_got(r2[p].at[s], rs_r.at[p, 1, s])
        i = place[order[1]]
        term = total(e_[p][pl.ds(pl.multiple_of(i * own, 16), own), :], [r2[p][s] for s in range(3)])
        i = place[order[2]]
        r3[p][i] = term
        for s in (1, 2, 3):
            ref = r3[p].at[i]
            start_copy(ref, ref, rs_s.at[p, 2, s - 1], rs_r.at[p, 2, s - 1], on_axis(order[2], s))

    def image_t3(c):
        if c < DETOUR:
            pl.when(jnp.logical_not(hand_down))(lambda: got(lambda r: t3.at[r], lambda m: tr3.at[m], no_forward)(c))
        else:
            got(lambda r: t3.at[r], lambda m: tr3.at[m], no_forward)(c)
        image_logits(c, t3, (((g + 7) % 8) * 16 + (k + 15) % 16) * ROWS)

    pl.when(outer_even)(lambda: add_grad(g_image, t2, False))
    pl.when(jnp.logical_not(outer_even))(lambda: image_t3(0))

    def block(p, a, b, c):
        base, own, _ = PARTS[p]
        if a is None:
            rows = pl.ds(base, 16 * own)
        elif b is None:
            rows = pl.ds(pl.multiple_of(base + a * 4 * own, 16), 4 * own)
        else:
            rows = pl.ds(pl.multiple_of(base + (a * 4 + b) * own, 16), own)
        if c is None:
            cols = pl.ds(mine, HALF)
        else:
            cols = pl.ds(pl.multiple_of(mine + c * 128, 128), 128)
        return rows, cols

    def gather(p, stage, rows, cols):
        axis = PARTS[p][2][stage]
        for s in (1, 2, 3):
            ref = out_ref.at[rows, cols]
            start_copy(ref, ref, ag_s.at[p, stage, s - 1], ag_r.at[p, stage, s - 1], on_axis(axis, s))

    def seat(p):
        order = PARTS[p][2]
        return [place[a] for a in order]

    for p in range(3):
        a, b, c = seat(p)
        for s in (1, 2, 3):
            wait_got(r3[p].at[(c - s + 4) % 4], rs_r.at[p, 2, s - 1])
        rows, cols = block(p, a, b, None)
        out_ref[rows, cols] = total(r3[p][0], [r3[p][s] for s in (1, 2, 3)])
        gather(p, 1, rows, cols)
    pl.when(outer_even)(lambda: image_t3(0))
    image_t3(1)
    for p in range(3):
        a, b, c = seat(p)
        for s in (1, 2, 3):
            wait_got(out_ref.at[block(p, a, (b - s + 4) % 4, None)], ag_r.at[p, 1, s - 1])
        gather(p, 0, *block(p, a, None, None))
        ref = out_ref.at[block(p, a, None, None)]
        start_copy(ref, ref, a0s.at[p, 0], a0r.at[p, 0], other_core)

    image_t3(2)
    add_grad(g_image, t3, False)

    def finish_image(c, _):
        r = pl.ds(pl.multiple_of(c * SEND, SEND), SEND)
        u = pic[r, :]
        inv = lax.rsqrt(jnp.sum(u * u, axis=1, keepdims=True) + EPS)
        u = u * inv
        v = g_image[r, :] * scale
        dot = jnp.sum(u * v, axis=1, keepdims=True)
        gi_ref[r, :] = ((v - u * dot) * inv).astype(BF16)
        return 0

    lax.fori_loop(0, SENDS, finish_image, 0)

    for p in range(3):
        a, b, c = seat(p)
        for s in (1, 2, 3):
            ref = out_ref.at[block(p, (a - s + 4) % 4, None, None)]
            wait_got(ref, ag_r.at[p, 0, s - 1])
            start_copy(ref, ref, a0s.at[p, s], a0r.at[p, s], other_core)
    for p in range(3):
        base, own, _ = PARTS[p]
        a, b, c = seat(p)
        for s in range(4):
            rows = pl.ds(pl.multiple_of(base + ((a - s + 4) % 4) * 4 * own, 16), 4 * own)
            wait_got(out_ref.at[rows, pl.ds(theirs, HALF)], a0r.at[p, s])

    wait_sent(idx, xs2)
    wait_sent(idx, xs3)

    def drain(c, _):
        r = pl.ds(pl.multiple_of(c * SEND, SEND), SEND)
        away = jnp.logical_or(
            jnp.logical_and(late_row, c < DETOUR * per), jnp.logical_and(last_odd, c < DETOUR_BACK * per)
        )
        handed = jnp.logical_or(
            jnp.logical_and(z == 1, c < DETOUR * per), jnp.logical_and(hand_back, c < DETOUR_BACK * per)
        )

        @pl.when(jnp.logical_not(away))
        def _():
            wait_sent(tu.at[r], ts2.at[c])

        @pl.when(jnp.logical_or(odd, z != 3))
        def _():
            wait_sent(iu.at[r], is2.at[c])

        @pl.when(direct_image)
        def _():
            wait_sent(iu.at[r], is3.at[c])

        @pl.when(direct_text)
        def _():
            wait_sent(tu.at[r], ts3.at[c])

        @pl.when(forward_image)
        def _():
            wait_sent(images.at[0, r], is3r.at[c])

        @pl.when(jnp.logical_or(forward_text, jnp.logical_and(first_even, c >= DETOUR * per)))
        def _():
            wait_sent(t2.at[r], ts3r.at[c])

        @pl.when(away)
        def _():
            wait_sent(tu.at[r], txs.at[c])

        @pl.when(handed)
        def _():
            wait_sent(tx.at[r], txf.at[c])

        return 0

    lax.fori_loop(0, SENDS, drain, 0)
    for p in range(3):
        base, own, _ = PARTS[p]
        a, b, c = seat(p)
        wait_sent(hs.at[span(p)], s0s.at[p])
        for s in range(3):
            wait_sent(r1[p].at[s], rs_s.at[p, 0, s])
            wait_sent(r2[p].at[s], rs_s.at[p, 1, s])
            wait_sent(r3[p].at[s], rs_s.at[p, 2, s])
            wait_sent(out_ref.at[block(p, a, b, None)], ag_s.at[p, 1, s])
            wait_sent(out_ref.at[block(p, a, None, None)], ag_s.at[p, 0, s])
        for s in range(4):
            wait_sent(out_ref.at[block(p, (a - s + 4) % 4, None, None)], a0s.at[p, s])


def scratch():
    vmem = pltpu.VMEM
    dma = pltpu.SemaphoreType.DMA
    block = vmem((ROWS, E), BF16)
    wide = vmem((ROWS, E), F32)
    index = vmem((8, ROWS), jnp.int32)
    owns = [own for _, own, _ in PARTS]
    return [
        pltpu.SMEM((1,), F32), pltpu.SMEM((1,), F32), vmem((ROWS,), jnp.int32), wide, vmem((ROWS, FT), BF16), vmem((FT, E), BF16), block, block, wide, vmem((ROWS, 128), F32), vmem((FT, ROWS), BF16),
        vmem((2, ROWS, E), BF16), block, block, block, index, vmem((2, 8, ROWS), jnp.int32), vmem((ROWS, 128), jnp.int32),
        vmem((ROWS, ROWS), BF16), wide, wide, block, vmem((FT, HALF), BF16), vmem((FT, HALF), BF16), vmem((FT, HALF), BF16),
        *[vmem((3, 4 * own, HALF), BF16) for own in owns],
        *[vmem((4 * own, HALF), BF16) for own in owns],
        *[vmem((3, own, HALF), BF16) for own in owns],
        *[vmem((4, own, HALF), BF16) for own in owns],
        dma((SENDS + 5,)),
        *[dma((SENDS,)) for _ in range(3)], dma((2 * SENDS,)), *[dma((SENDS,)) for _ in range(8)],
        dma, dma, dma((2,)),
        dma((3,)), dma((3,)), dma((3, 3, 3)), dma((3, 3, 3)), dma((3, 3, 3)), dma((3, 3, 3)), dma((3, 4)), dma((3, 4)),
    ]


def widen(a_ref, b_ref, a_out, b_out, a_wide, b_wide, sem):
    copies = []
    for ref, out, wide, first in ((b_ref, b_out, b_wide, 0), (a_ref, a_out, a_wide, FT // TILE)):
        for c in range(ref.shape[0] // TILE):
            r = pl.ds(c * TILE, TILE)
            wide[r, :] = ref[r, :].astype(F32)
            copies.append(pltpu.make_async_copy(wide.at[r], out.at[r], sem.at[first + c]))
            copies[-1].start()
    for copy in copies:
        copy.wait()


def on_device(
    picture_embedding_unscaled,
    caption_tower_outputs,
    caption_mapping_matrix,
    matching_caption_index,
    similarity_scaling,
    score_offset,
):
    vmem = pl.BlockSpec(memory_space=pltpu.VMEM)
    anywhere = pl.BlockSpec(memory_space=pl.ANY)
    grad_image, grad_proj = pl.pallas_call(
        kernel,
        out_shape=(jax.ShapeDtypeStruct((ROWS, E), BF16), jax.ShapeDtypeStruct((FT, E), BF16)),
        in_specs=[pl.BlockSpec(memory_space=pltpu.HBM)] * 6,
        out_specs=(vmem, vmem),
        scratch_shapes=scratch(),
        compiler_params=pltpu.CompilerParams(
            collective_id=0, has_side_effects=True, vmem_limit_bytes=48 * 1024 * 1024
        ),
    )(
        similarity_scaling, score_offset,
        *[pltpu.with_memory_space_constraint(a, pltpu.HBM) for a in (
            matching_caption_index, picture_embedding_unscaled, caption_tower_outputs, caption_mapping_matrix,
        )],
    )
    return pl.pallas_call(
        widen,
        out_shape=(jax.ShapeDtypeStruct((ROWS, E), F32), jax.ShapeDtypeStruct((FT, E), F32)),
        in_specs=[vmem, vmem],
        out_specs=(anywhere, anywhere),
        scratch_shapes=[
            pltpu.VMEM((ROWS, E), F32), pltpu.VMEM((FT, E), F32), pltpu.SemaphoreType.DMA(((ROWS + FT) // TILE,)),
        ],
        compiler_params=pltpu.CompilerParams(vmem_limit_bytes=16 * 1024 * 1024),
    )(grad_image, grad_proj)


def solution(mesh):
    return jax.shard_map(
        on_device,
        mesh=mesh,
        in_specs=(
            P(("group", "blk"), None),
            P(("group", "blk"), None),
            P(),
            P(("group", "blk")),
            P(),
            P(),
        ),
        out_specs=(P(("group", "blk"), None), P()),
        check_vma=False,
    )
```
